512 devices in a mesh: seq: 32 (over x_lo, z), exp: 8 (over y, core), batch: 2 (over x_hi).
Axes of the slice: x: 4 (x_hi: 2, x_lo: 2; x = x_hi * 2 + x_lo), y: 4, z: 16, core: 2. Of those that a mesh axis runs over, the one named last changes fastest.
Arguments:
- queries: bfloat16 [2, 4096, 2048], P('batch', 'seq', 'exp'), may hold values from -100 to 100
- keys_values: bfloat16 [2, 4096, 1024], P('batch', 'seq', 'exp'), may hold values from -10 to 10
- sinks: float32 [32], P('exp'), may hold values from -1 to 4
- out_weight: bfloat16 [2048, 2880], P('exp'), may hold values from -0.25 to 0.25
- hidden_in: bfloat16 [2, 4096, 2880], P('batch', ('seq', 'exp')), may hold values from -3 to 3
- norm_gain: float32 [2880], replicated, may hold values from 0.1 to 1.9
- expert_ids: int32 [2, 4096, 4], P('batch', 'seq'), may hold values from 0 to 31, all different within a row; in each aligned block of 128 rows (0 to 127, 128 to 255, ..., all dimensions but the last counted through in order) at most 24 rows name the same one
- expert_gates: bfloat16 [2, 4096, 4], P('batch', 'seq'), may hold values from 0.099609375 to 0.59765625
- gate_weight: bfloat16 [32, 2880, 1440], P('seq', None, 'exp'), may hold values from -0.109375 to 0.109375
- up_weight: bfloat16 [32, 2880, 1440], P('seq', None, 'exp'), may hold values from -0.109375 to 0.109375
- down_weight: bfloat16 [32, 1440, 2880], P('seq', 'exp'), may hold values from -0.15625 to 0.15625
Outputs:
- layer_out: bfloat16 [2, 4096, 2880], P('batch', ('seq', 'exp'))
The draws below stay inside these ranges and needn't reach their ends.
Inputs may be any that keep to these rules, and one draw needn't show every extreme that they name: `expert_ids`: each token names 4 different experts. In each block of 128 positions of a sequence no expert is named by more than 24 tokens, and in some block one expert is named by exactly 24.
All inputs are finite; a program needn't handle non-finite values.
Results may differ from the reference program's by a relative error of at most 0.015.
Values may be sent and summed in bfloat16 or wider, within the bound.
No kernel may reach another device: no remote copies, remote signals or barrier semaphores. Data moves between devices by JAX's collectives and lax.ppermute only.
A program may use at most 64 MiB of HBM per device.

```python
import math
import jax
import jax.numpy as jnp
import numpy as np
from jax import lax

D = 2880
FF = 1440
HEADS = 32
KV_HEADS = 8
HEAD = 64
TOP = 4
BLK = 128
SEQ_LEN = 4096
EXPERTS = 32
FF_DEV = 180
CAP = 24
N_SEQ = 32
N_EXP = 8


def base_pair(key):
    first_key, second_key = jax.random.split(key)
    query = jnp.clip(2.0 * jax.random.normal(first_key, (2, SEQ_LEN, HEADS, HEAD), jnp.float32), -9.0, 9.0)
    paired = jnp.clip(jax.random.normal(second_key, (2, SEQ_LEN, KV_HEADS, 2, HEAD), jnp.float32), -4.5, 4.5)
    return (query, paired)


def draw_queries(key, part):
    query, paired = base_pair(key)
    return query.reshape(2, SEQ_LEN, HEADS * HEAD).astype(jnp.bfloat16)


def draw_keys_values(key, part):
    query, paired = base_pair(key)
    return paired.reshape(2, SEQ_LEN, KV_HEADS * 2 * HEAD).astype(jnp.bfloat16)


def level_of(key, extent, pieces, least, top_value):
    def one(dim, parts):
        draws = jax.random.uniform(jax.random.fold_in(jax.random.fold_in(key, 6), dim), (parts,), jnp.float32, least / len(pieces), top_value / len(pieces))
        return jnp.repeat(jnp.exp(draws), extent[dim] // parts).reshape((-1,) + (1,) * (len(extent) - dim - 1))

    level = one(*pieces[0])
    for cut in pieces[1:]:
        level = level * one(*cut)
    return level


def routed_block(stream_key, own, number, rows, count, top, bound, skew):
    order = jax.random.permutation(stream_key, count)
    heavy_load, common = load_shares(count, rows * top, bound, skew, True), load_shares(count, rows * top, bound, skew, False)
    places = jnp.arange(count)

    def named(lengths, turn):
        used = int((lengths > 0).sum())
        fixed = max(1, used // 4)
        shifted = fixed + (places - fixed + turn * (used - fixed)) % max(1, count - fixed)
        return jnp.zeros((count,), jnp.int32).at[order[jnp.where(places < fixed, places, shifted)]].set(jnp.asarray(lengths, jnp.int32))

    lengths = jnp.where(number % 4 == 0, named(heavy_load, number // 4), named(common, number - number // 4 - 1))
    mixed = jax.random.permutation(jax.random.fold_in(own, 3), count)
    source_of, receiver = mixed[0:count // 2 * 2:2], mixed[1:count // 2 * 2:2]
    room = jnp.minimum(lengths[source_of] - 1, bound - lengths[receiver]) // 2
    room = jnp.where((source_of == order[0]) | (receiver == order[0]) | (lengths[receiver] == 0), 0, jnp.maximum(room, 0))
    shifted = jax.random.randint(jax.random.fold_in(own, 4), (count // 2,), 0, 1 << 20) % (room + 1)
    lengths = lengths.at[source_of].add(-shifted).at[receiver].add(shifted)
    items = jnp.searchsorted(jnp.cumsum(lengths), jnp.arange(rows * top), side="right").astype(jnp.int32)
    listing = items.reshape(top, rows).T
    listing = listing[jax.random.permutation(jax.random.fold_in(own, 1), rows)]
    turn = jax.random.randint(jax.random.fold_in(own, 2), (rows, 1), 0, top)
    return jnp.take_along_axis(listing, (jnp.arange(top)[None, :] + turn) % top, axis=1)


def load_shares(count, total, reach, slope, full):
    loads = [(1 << 20) // math.isqrt(standing ** slope) + 1 for standing in range(1, count + 1)]
    largest = reach if full else min(reach, max(-(-total // count), total * loads[0] // sum(loads)))
    least = 1 if total - largest >= count - 1 else 0
    counts, rest = [largest] + [least] * (count - 1), total - largest - least * (count - 1)
    while rest > 0:
        candidates = [i for i in range(1, count) if counts[i] < largest] or [i for i in range(1, count) if counts[i] < reach]
        mass, left = sum([loads[i] for i in candidates]), rest
        for i in candidates:
            extra = min(reach - counts[i], max(1, left * loads[i] // mass), rest)
            counts[i] = counts[i] + extra
            rest = rest - extra
    return np.array(counts)


def gaussian(key, extent, spread, bound, shards=(), kind=jnp.bfloat16):
    values = spread * jax.random.normal(key, extent, jnp.float32)
    if shards:
        values = values * level_of(key, extent, shards, -0.22, 0.18)
    return jnp.clip(values, -bound, bound).astype(kind)


def setup_inputs(seed: int = 0) -> dict:
    key_of = jax.random.split(jax.random.key(seed), 12)
    queries = draw_queries(jax.random.fold_in(key_of[11], 71), 0)
    keys_values = draw_keys_values(jax.random.fold_in(key_of[11], 71), 0)
    sinks = jnp.clip(-1.0 + 5.0 * jax.random.uniform(key_of[2], (HEADS,), jnp.float32) ** level_of(key_of[2], (HEADS,), ((0, 8),), -0.2, 0.2), -1.0, 4.0)
    out_weight = gaussian(key_of[3], (HEADS * HEAD, D), (KV_HEADS * HEAD) ** -0.5, 0.25, ((0, 8),))
    hidden_in = gaussian(key_of[4], (2, SEQ_LEN, D), 0.5, 3.0, ((0, 2), (1, 256)))
    norm_gain = jnp.clip(1.0 + 0.18 * jax.random.normal(key_of[5], (D,), jnp.float32), 0.1, 1.9)
    expert_ids_keys = jax.random.split(jax.random.fold_in(key_of[6], 1), 2 * SEQ_LEN // BLK)
    expert_ids_turns = jax.random.permutation(jax.random.fold_in(key_of[6], 3), 2 * SEQ_LEN // BLK)
    expert_ids = jax.vmap(lambda own, number: routed_block(jax.random.fold_in(key_of[6], 2), own, number, BLK, EXPERTS, TOP, CAP, 2))(expert_ids_keys, expert_ids_turns).reshape((2, SEQ_LEN, TOP))
    expert_gates = jnp.clip(0.099609375 + 0.49804688 * jax.random.uniform(key_of[7], (2, SEQ_LEN, TOP), jnp.float32) ** level_of(key_of[7], (2, SEQ_LEN, TOP), ((0, 2), (1, 32)), -0.2, 0.2), 0.099609375, 0.59765625).astype(jnp.bfloat16)
    gate_weight = gaussian(key_of[8], (EXPERTS, D, FF), D ** -0.5, 0.109375, ((0, 32), (2, 8)))
    up_weight = gaussian(key_of[9], (EXPERTS, D, FF), D ** -0.5, 0.109375, ((0, 32), (2, 8)))
    down_weight = gaussian(key_of[10], (EXPERTS, FF, D), FF ** -0.5, 0.15625, ((0, 32), (1, 8)))
    return {"queries": queries, "keys_values": keys_values, "sinks": sinks, "out_weight": out_weight, "hidden_in": hidden_in, "norm_gain": norm_gain, "expert_ids": expert_ids, "expert_gates": expert_gates, "gate_weight": gate_weight, "up_weight": up_weight, "down_weight": down_weight}


def attend_block(query_block, first_pos, pair_rows, sink_grid):
    row_count = query_block.shape[0]
    key_rows = pair_rows[:, :, 0, :].astype(jnp.float32)
    value_rows = pair_rows[:, :, 1, :].astype(jnp.float32)
    scores = jnp.einsum('rkgd,jkd->kgrj', query_block.astype(jnp.float32), key_rows) * 0.125
    query_pos = first_pos + jnp.arange(row_count, dtype=jnp.int32)
    key_pos = jnp.arange(SEQ_LEN, dtype=jnp.int32)
    allowed = key_pos[None, :] <= query_pos[:, None]
    scores = jnp.where(allowed, scores, -1e+30)
    largest = jnp.maximum(lax.optimization_barrier(jnp.max(scores, axis=-1)), sink_grid[:, :, None])
    numerators = jnp.exp(scores - largest[..., None])
    totals = lax.optimization_barrier(jnp.sum(numerators, axis=-1)) + jnp.exp(sink_grid[:, :, None] - largest)
    weights = numerators.astype(jnp.bfloat16)
    mixed = jnp.einsum('kgrj,jkd->kgrd', weights.astype(jnp.float32), value_rows) / totals[..., None]
    mixed = mixed.astype(jnp.bfloat16)
    return mixed.transpose(2, 0, 1, 3).reshape(row_count, HEADS * HEAD)

def reference(queries, keys_values, sinks, out_weight, hidden_in, norm_gain, expert_ids, expert_gates, gate_weight, up_weight, down_weight):
    group_size = HEADS // KV_HEADS
    block_size = 256 if SEQ_LEN % 256 == 0 else SEQ_LEN
    block_total = SEQ_LEN // block_size
    sink_grid = sinks.reshape(KV_HEADS, group_size).astype(jnp.float32)
    outputs = []
    for member in range(2):
        query_blocks = queries[member].reshape(block_total, block_size, KV_HEADS, group_size, HEAD)
        pair_rows = keys_values[member].reshape(SEQ_LEN, KV_HEADS, 2, HEAD)

        def one_block(item):
            return attend_block(item[0], item[1] * block_size, pair_rows, sink_grid)
        mixed = lax.map(one_block, (query_blocks, jnp.arange(block_total, dtype=jnp.int32)))
        outputs.append(mixed.reshape(SEQ_LEN, HEADS * HEAD))
    heads_out = jnp.concatenate(outputs, axis=0)
    attention = jnp.dot(heads_out, out_weight, preferred_element_type=jnp.float32)
    residual = (hidden_in.reshape(2 * SEQ_LEN, D).astype(jnp.float32) + attention).astype(jnp.bfloat16)
    stream = residual.astype(jnp.float32)
    mean_square = lax.optimization_barrier(jnp.mean(stream * stream, axis=-1, keepdims=True))
    normed = (stream * lax.rsqrt(mean_square + 1e-05) * norm_gain.astype(jnp.float32)).astype(jnp.bfloat16)
    flat_ids = expert_ids.reshape(2 * SEQ_LEN, TOP)
    flat_gates = expert_gates.reshape(2 * SEQ_LEN, TOP).astype(jnp.float32)
    most_rows = 2 * N_SEQ * CAP

    def one_expert(total, item):
        gate_matrix, up_matrix, down_matrix, number = item
        matches = flat_ids == number
        used = jnp.any(matches, axis=1)
        factor = lax.optimization_barrier(jnp.sum(jnp.where(matches, flat_gates, jnp.zeros_like(flat_gates)), axis=1))
        picked = jnp.nonzero(used, size=most_rows, fill_value=0)[0]
        live = jnp.arange(most_rows) < jnp.sum(used.astype(jnp.int32))
        rows = normed[picked]
        gate = jnp.dot(rows, gate_matrix, preferred_element_type=jnp.float32)
        lifted = jnp.dot(rows, up_matrix, preferred_element_type=jnp.float32)
        hidden = (gate * jax.nn.sigmoid(1.702 * gate) * (lifted + 1.0)).astype(jnp.bfloat16)
        partials = jnp.einsum('rgf,gfd->rgd', hidden.reshape(most_rows, N_EXP, FF_DEV).astype(jnp.float32), down_matrix.reshape(N_EXP, FF_DEV, D).astype(jnp.float32))
        partials = partials.astype(jnp.bfloat16)
        output = lax.optimization_barrier(jnp.sum(partials.astype(jnp.float32), axis=1))
        scales = jnp.where(live, factor[picked], jnp.zeros_like(factor[picked]))
        return (total.at[picked].add(output * scales[:, None]), None)
    expert_sum, unused = lax.scan(one_expert, jnp.zeros((2 * SEQ_LEN, D), jnp.float32), (gate_weight, up_weight, down_weight, jnp.arange(EXPERTS, dtype=jnp.int32)))
    layer_out = (stream + expert_sum).astype(jnp.bfloat16)
    return layer_out.reshape(2, SEQ_LEN, D)
```

```python
import functools

import jax
import jax.numpy as jnp
from jax import lax
from jax.experimental import pallas as pl
from jax.experimental.pallas import tpu as pltpu
from jax.sharding import PartitionSpec as P

HEAD = 64
HALF = 192


def expert_kernel(rows_ref, lift_ref, down_ref, out_ref, total_ref):
    step = pl.program_id(0)
    units = down_ref.shape[1]
    both = jnp.dot(rows_ref[...], lift_ref[0], preferred_element_type=jnp.float32)
    gate = both[:, :units]
    lifted = both[:, HALF : HALF + units]
    hidden = (gate * jax.nn.sigmoid(1.702 * gate) * (lifted + 1.0)).astype(jnp.bfloat16)
    term = jnp.dot(hidden, down_ref[0], preferred_element_type=jnp.float32)

    @pl.when(step == 0)
    def _():
        total_ref[...] = term

    @pl.when(step > 0)
    def _():
        total_ref[...] += term

    @pl.when(step == pl.num_programs(0) - 1)
    def _():
        out_ref[...] = total_ref[...].astype(out_ref.dtype)


def run_expert(rows, lift, down):
    count, width = rows.shape
    groups, units, _ = down.shape
    return pl.pallas_call(
        expert_kernel,
        grid=(groups,),
        in_specs=[
            pl.BlockSpec((count, width), lambda g: (0, 0)),
            pl.BlockSpec((1, width, 2 * HALF), lambda g: (g, 0, 0)),
            pl.BlockSpec((1, units, width), lambda g: (g, 0, 0)),
        ],
        out_specs=pl.BlockSpec((count, width), lambda g: (0, 0)),
        out_shape=jax.ShapeDtypeStruct((count, width), jnp.bfloat16),
        scratch_shapes=[pltpu.VMEM((count, width), jnp.float32)],
        compiler_params=pltpu.CompilerParams(vmem_limit_bytes=40 * 1024 * 1024),
        cost_estimate=pl.CostEstimate(
            flops=6 * count * width * units * groups,
            bytes_accessed=groups * (2 * HALF + units) * width * 2,
            transcendentals=count * units * groups,
        ),
    )(rows, lift, down)


def on_device(
    queries,
    keys_values,
    sinks,
    out_weight,
    hidden_in,
    norm_gain,
    expert_ids,
    expert_gates,
    gate_weight,
    up_weight,
    down_weight,
):
    seq_devices = lax.axis_size("seq")
    exp_devices = lax.axis_size("exp")
    block_rows = queries.shape[1]
    heads = sinks.shape[0]
    width = out_weight.shape[1]
    own_rows = hidden_in.shape[1]
    units = gate_weight.shape[2]
    seq_rank = lax.axis_index("seq")
    exp_rank = lax.axis_index("exp")

    with jax.named_scope("gather_weights"):
        zeros = jnp.zeros((width, HALF - units), jnp.bfloat16)
        lift_own = jnp.concatenate([gate_weight[0], zeros, up_weight[0], zeros], axis=1)
        lift_all = lax.all_gather(lift_own, "exp", axis=0, tiled=False)
        down_all = lax.all_gather(down_weight[0], "exp", axis=0, tiled=False)

    with jax.named_scope("gather_keys"):
        copies = jnp.broadcast_to(keys_values, (seq_devices,) + keys_values.shape[1:])
        pairs = lax.all_to_all(copies, "seq", split_axis=0, concat_axis=0, tiled=True)
        pairs = pairs.reshape(seq_devices * block_rows, 2 * HEAD)

    with jax.named_scope("attend"):
        grid = queries[0].reshape(block_rows, heads, HEAD)
        scores = (
            jnp.einsum("igd,jd->gij", grid, pairs[:, :HEAD], preferred_element_type=jnp.float32)
            * 0.125
        )
        query_pos = seq_rank * block_rows + jnp.arange(block_rows, dtype=jnp.int32)
        key_pos = jnp.arange(seq_devices * block_rows, dtype=jnp.int32)
        scores = jnp.where(key_pos[None, :] <= query_pos[:, None], scores, -1e30)
        largest = jnp.maximum(jnp.max(scores, axis=-1), sinks[:, None])
        numerators = jnp.exp(scores - largest[..., None])
        totals = jnp.sum(numerators, axis=-1) + jnp.exp(sinks[:, None] - largest)
        weighted = jnp.einsum(
            "gij,jd->gid",
            numerators.astype(jnp.bfloat16),
            pairs[:, HEAD:],
            preferred_element_type=jnp.float32,
        )
        mixed = (weighted / totals[..., None]).astype(jnp.bfloat16)
        heads_out = mixed.transpose(1, 0, 2).reshape(block_rows, heads * HEAD)

    with jax.named_scope("project"):
        head_term = jnp.dot(heads_out, out_weight, preferred_element_type=jnp.float32)
        head_parts = head_term.astype(jnp.bfloat16).reshape(exp_devices, own_rows, width)
        own_parts = lax.all_to_all(head_parts, "exp", split_axis=0, concat_axis=0, tiled=True)
        attention = jnp.sum(own_parts.astype(jnp.float32), axis=0)
        residual = (hidden_in[0].astype(jnp.float32) + attention).astype(jnp.bfloat16)

    with jax.named_scope("norm"):
        stream = residual.astype(jnp.float32)
        mean_square = jnp.mean(stream * stream, axis=-1, keepdims=True)
        normed_own = (stream * lax.rsqrt(mean_square + 1e-05) * norm_gain).astype(jnp.bfloat16)
        normed = lax.all_gather(normed_own, "exp", axis=0, tiled=True)

    with jax.named_scope("route"):
        chosen = expert_ids[0]
        top_count = chosen.shape[1]
        share = (3 * block_rows * top_count + 2 * seq_devices * exp_devices - 1) // (
            2 * seq_devices * exp_devices
        )
        hits = (chosen[:, :, None] == jnp.arange(seq_devices, dtype=jnp.int32)).astype(jnp.float32)
        token_hits = jnp.sum(hits, axis=1)
        earlier = (
            jnp.arange(block_rows)[:, None] > jnp.arange(block_rows)[None, :]
        ).astype(jnp.float32)
        slots = jnp.dot(earlier, token_hits)
        wanted = (exp_rank * share + jnp.arange(share, dtype=jnp.int32)).astype(jnp.float32)
        picks = (token_hits[:, :, None] > 0) & (slots[:, :, None] == wanted)
        selector = picks.astype(jnp.bfloat16)
        factor = jnp.einsum("tke,tk->te", hits, expert_gates[0].astype(jnp.float32))
        combiner = jnp.where(picks, factor[:, :, None], 0.0).astype(jnp.bfloat16)
        combiner = combiner.reshape(block_rows, seq_devices * share)

    with jax.named_scope("dispatch"):
        outgoing = jnp.einsum(
            "tec,td->ecd", selector, normed, preferred_element_type=jnp.float32
        ).astype(jnp.bfloat16)
        arrived = lax.all_to_all(outgoing, "seq", split_axis=0, concat_axis=0, tiled=True)

    with jax.named_scope("experts"):
        arrived_rows = arrived.reshape(seq_devices * share, width)
        done = run_expert(arrived_rows, lift_all, down_all)

    with jax.named_scope("combine"):
        returned = lax.all_to_all(
            done.reshape(seq_devices, share, width), "seq", split_axis=0, concat_axis=0, tiled=True
        )
        mixed_rows = jnp.dot(
            combiner,
            returned.reshape(seq_devices * share, width),
            preferred_element_type=jnp.float32,
        )
        term = mixed_rows.astype(jnp.bfloat16).reshape(exp_devices, own_rows, width)
        terms = lax.all_to_all(term, "exp", split_axis=0, concat_axis=0, tiled=True)
        expert_sum = jnp.sum(terms.astype(jnp.float32), axis=0)
        layer_out = (residual.astype(jnp.float32) + expert_sum).astype(jnp.bfloat16)
    return layer_out[None]


def solution(mesh):
    placed = (
        P("batch", "seq", "exp"),
        P("batch", "seq", "exp"),
        P("exp"),
        P("exp", None),
        P("batch", ("seq", "exp"), None),
        P(),
        P("batch", "seq", None),
        P("batch", "seq", None),
        P("seq", None, "exp"),
        P("seq", None, "exp"),
        P("seq", "exp", None),
    )
    return jax.shard_map(
        on_device,
        mesh=mesh,
        in_specs=placed,
        out_specs=P("batch", ("seq", "exp"), None),
        check_vma=False,
    )
```

```python
import jax
import jax.numpy as jnp
from jax import lax
from jax.experimental import pallas as pl
from jax.experimental.pallas import tpu as pltpu
from jax.sharding import PartitionSpec as P

HEAD = 64
LIFT_ROWS = 368
CHUNK = 384
CAP = 24
RUN = 16


def pack_kernel(gate_ref, up_ref, down_ref, out_ref):
    units, width = gate_ref.shape
    spare = jnp.zeros((LIFT_ROWS - 2 * units, width), out_ref.dtype)
    out_ref[...] = jnp.concatenate([gate_ref[...], up_ref[...], spare, down_ref[...]], axis=0)


def pack_weights(gate_across, up_across, down):
    units, width = down.shape
    depth = LIFT_ROWS + units
    return pl.pallas_call(
        pack_kernel,
        out_shape=jax.ShapeDtypeStruct((depth, width), down.dtype),
        compiler_params=pltpu.CompilerParams(vmem_limit_bytes=24 * 1024 * 1024),
        cost_estimate=pl.CostEstimate(
            flops=0, bytes_accessed=4 * depth * width, transcendentals=0
        ),
    )(gate_across, up_across, down)


def expert_kernel(rows_ref, weight_ref, out_ref, total_ref):
    step = pl.program_id(0)
    units = weight_ref.shape[1] - LIFT_ROWS
    cut = LIFT_ROWS // 32 * 16
    rows = rows_ref[...]
    both = jnp.concatenate(
        [
            jnp.dot(weight_ref[0, :cut, :], rows, preferred_element_type=jnp.float32),
            jnp.dot(weight_ref[0, cut:LIFT_ROWS, :], rows, preferred_element_type=jnp.float32),
        ],
        axis=0,
    )
    gate = both[:units]
    lifted = both[units : 2 * units]
    hidden = gate * jax.nn.sigmoid(1.702 * gate) * (lifted + 1.0)

    @pl.when(step == 0)
    def _():
        total_ref[...] = jnp.zeros_like(total_ref)

    total_ref[...] += jnp.dot(
        hidden.T.astype(jnp.bfloat16),
        weight_ref[0, LIFT_ROWS:, :],
        preferred_element_type=jnp.float32,
    )

    @pl.when(step == pl.num_programs(0) - 1)
    def _():
        count, width = total_ref.shape
        chunks = out_ref.shape[0] // count
        part = 24
        side = part * chunks
        share = CAP // chunks
        row = lax.broadcasted_iota(jnp.int32, (side, side), 0)
        col = lax.broadcasted_iota(jnp.int32, (side, side), 1)
        block, rest = row // (chunks * share), row % (chunks * share)
        source = (rest // share) * part + block * share + rest % share
        turn = (source == col).astype(jnp.bfloat16)
        for first in range(0, count, part):
            pieces = []
            for chunk in range(chunks):
                low, high = chunk * CHUNK, min((chunk + 1) * CHUNK, width)
                piece = total_ref[first : first + part, low:high]
                if high - low < CHUNK:
                    fill = jnp.zeros((part, CHUNK - (high - low)), jnp.float32)
                    piece = jnp.concatenate([piece, fill], axis=1)
                pieces.append(piece)
            stacked = jnp.concatenate(pieces, axis=0).astype(jnp.bfloat16)
            out_ref[first * chunks : (first + part) * chunks, :] = jnp.dot(
                turn, stacked, preferred_element_type=jnp.float32
            ).astype(out_ref.dtype)


def run_expert(rows_across, weights):
    width, count = rows_across.shape
    groups, depth, _ = weights.shape
    chunks = -(-width // CHUNK)
    return pl.pallas_call(
        expert_kernel,
        grid=(groups,),
        in_specs=[
            pl.BlockSpec((width, count), lambda g: (0, 0)),
            pl.BlockSpec((1, depth, width), lambda g: (g, 0, 0)),
        ],
        out_specs=pl.BlockSpec((count * chunks, CHUNK), lambda g: (0, 0)),
        out_shape=jax.ShapeDtypeStruct((count * chunks, CHUNK), jnp.bfloat16),
        scratch_shapes=[pltpu.VMEM((count, width), jnp.float32)],
        compiler_params=pltpu.CompilerParams(vmem_limit_bytes=40 * 1024 * 1024),
        cost_estimate=pl.CostEstimate(
            flops=2 * count * width * depth * groups,
            bytes_accessed=groups * depth * width * 2,
            transcendentals=count * depth * groups // 3,
        ),
    )(rows_across, weights)


def on_device(
    queries,
    keys_values,
    sinks,
    out_weight,
    hidden_in,
    norm_gain,
    expert_ids,
    expert_gates,
    gate_weight,
    up_weight,
    down_weight,
):
    seq_devices = lax.axis_size("seq")
    exp_devices = lax.axis_size("exp")
    block_rows = queries.shape[1]
    heads = sinks.shape[0]
    width = out_weight.shape[1]
    own_rows = hidden_in.shape[1]
    units = gate_weight.shape[2]
    seq_rank = lax.axis_index("seq")
    exp_rank = lax.axis_index("exp")
    run_rows = RUN * block_rows
    runs = seq_devices // RUN

    with jax.named_scope("gather_weights"):
        weights = lax.all_gather(
            pack_weights(gate_weight[0].T, up_weight[0].T, down_weight[0]),
            "exp",
            axis=0,
            tiled=False,
        )

    with jax.named_scope("gather_keys"):
        run_groups = [[r * RUN + i for i in range(RUN)] for r in range(runs)]
        copies = jnp.broadcast_to(keys_values, (RUN,) + keys_values.shape[1:])
        near = lax.all_to_all(
            copies, "seq", split_axis=0, concat_axis=0, tiled=True, axis_index_groups=run_groups
        )
        near = near.reshape(run_rows, 2 * HEAD)
        far = lax.ppermute(near, "seq", [(i, i + RUN) for i in range(seq_devices - RUN)])

    with jax.named_scope("attend"):
        grid = queries[0].reshape(block_rows, heads, HEAD)
        query_pos = seq_rank * block_rows + jnp.arange(block_rows, dtype=jnp.int32)
        first_near = (seq_rank // RUN) * run_rows
        offsets = jnp.arange(run_rows, dtype=jnp.int32)

        def score(keys, key_pos, keep):
            raw = (
                jnp.einsum("igd,jd->gij", grid, keys, preferred_element_type=jnp.float32) * 0.125
            )
            return jnp.where((key_pos[None, :] <= query_pos[:, None]) & keep, raw, -1e30)

        near_scores = score(near[:, :HEAD], first_near + offsets, True)
        far_scores = score(far[:, :HEAD], first_near - run_rows + offsets, seq_rank >= RUN)
        largest = jnp.maximum(
            jnp.maximum(jnp.max(near_scores, axis=-1), jnp.max(far_scores, axis=-1)),
            sinks[:, None],
        )
        near_top = jnp.exp(near_scores - largest[..., None])
        far_top = jnp.exp(far_scores - largest[..., None])
        totals = (
            jnp.sum(near_top, axis=-1)
            + jnp.sum(far_top, axis=-1)
            + jnp.exp(sinks[:, None] - largest)
        )
        weighted = jnp.einsum(
            "gij,jd->gid",
            near_top.astype(jnp.bfloat16),
            near[:, HEAD:],
            preferred_element_type=jnp.float32,
        ) + jnp.einsum(
            "gij,jd->gid",
            far_top.astype(jnp.bfloat16),
            far[:, HEAD:],
            preferred_element_type=jnp.float32,
        )
        mixed = (weighted / totals[..., None]).astype(jnp.bfloat16)
        heads_out = mixed.transpose(1, 0, 2).reshape(block_rows, heads * HEAD)

    with jax.named_scope("project"):
        head_term = jnp.dot(heads_out, out_weight, preferred_element_type=jnp.float32)
        head_parts = head_term.astype(jnp.bfloat16).reshape(exp_devices, own_rows, width)
        own_parts = lax.all_to_all(head_parts, "exp", split_axis=0, concat_axis=0, tiled=True)
        attention = jnp.sum(own_parts.astype(jnp.float32), axis=0)
        residual = (hidden_in[0].astype(jnp.float32) + attention).astype(jnp.bfloat16)

    with jax.named_scope("norm"):
        stream = residual.astype(jnp.float32)
        mean_square = jnp.mean(stream * stream, axis=-1, keepdims=True)
        normed_own = (stream * lax.rsqrt(mean_square + 1e-05) * norm_gain).astype(jnp.bfloat16)
        normed = lax.all_gather(normed_own, "exp", axis=0, tiled=True)

    with jax.named_scope("route"):
        chosen = expert_ids[0]
        share = CAP // exp_devices
        hits = (chosen[:, :, None] == jnp.arange(seq_devices, dtype=jnp.int32)).astype(jnp.float32)
        token_hits = jnp.sum(hits, axis=1)
        earlier = (
            jnp.arange(block_rows)[:, None] > jnp.arange(block_rows)[None, :]
        ).astype(jnp.float32)
        slots = jnp.dot(earlier, token_hits)
        named = token_hits[:, :, None] > 0
        wanted = (exp_rank * share + jnp.arange(share, dtype=jnp.int32)).astype(jnp.float32)
        picks = named & (slots[:, :, None] == wanted)
        selector = picks.astype(jnp.bfloat16)
        factor = jnp.einsum("tke,tk->te", hits, expert_gates[0].astype(jnp.float32))
        combiner = jnp.where(picks, factor[:, :, None], 0.0).astype(jnp.bfloat16)
        chunks = -(-width // CHUNK)
        by_owner = combiner.reshape(exp_devices, 1, own_rows, seq_devices, 1, share)
        same = jnp.eye(chunks, dtype=jnp.bfloat16).reshape(1, chunks, 1, 1, chunks, 1)
        combiner = (by_owner * same).reshape(
            exp_devices * chunks * own_rows, seq_devices * chunks * share
        )

    with jax.named_scope("dispatch"):
        outgoing = jnp.einsum(
            "tec,td->ecd", selector, normed, preferred_element_type=jnp.float32
        ).astype(jnp.bfloat16)
        arrived = lax.all_to_all(outgoing, "seq", split_axis=0, concat_axis=0, tiled=True)

    with jax.named_scope("experts"):
        rows_across = arrived.reshape(seq_devices * share, width).T
        done = run_expert(rows_across, weights)

    with jax.named_scope("combine"):
        returned = lax.all_to_all(
            done.reshape(seq_devices, chunks * share, CHUNK),
            "seq",
            split_axis=0,
            concat_axis=0,
            tiled=True,
        )
        mixed_rows = jnp.dot(
            combiner,
            returned.reshape(seq_devices * chunks * share, CHUNK),
            preferred_element_type=jnp.float32,
        )
        term = mixed_rows.astype(jnp.bfloat16).reshape(exp_devices, chunks * own_rows, CHUNK)
        terms = lax.all_to_all(term, "exp", split_axis=0, concat_axis=0, tiled=True)
        expert_sum = jnp.sum(terms.astype(jnp.float32), axis=0)
        expert_sum = expert_sum.reshape(chunks, own_rows, CHUNK).transpose(1, 0, 2)
        expert_sum = expert_sum.reshape(own_rows, chunks * CHUNK)[:, :width]
        layer_out = (residual.astype(jnp.float32) + expert_sum).astype(jnp.bfloat16)
    return layer_out[None]


def solution(mesh):
    placed = (
        P("batch", "seq", "exp"),
        P("batch", "seq", "exp"),
        P("exp"),
        P("exp", None),
        P("batch", ("seq", "exp"), None),
        P(),
        P("batch", "seq", None),
        P("batch", "seq", None),
        P("seq", None, "exp"),
        P("seq", None, "exp"),
        P("seq", "exp", None),
    )
    return jax.shard_map(
        on_device,
        mesh=mesh,
        in_specs=placed,
        out_specs=P("batch", ("seq", "exp"), None),
        check_vma=False,
    )
```

```python
import jax
import jax.numpy as jnp
from jax import lax
from jax.experimental import pallas as pl
from jax.experimental.pallas import tpu as pltpu
from jax.sharding import PartitionSpec as P

HEAD = 64
LIFT_ROWS = 368
CHUNK = 384
CAP = 24
GROUP = 24
CORES = 2
RUN = 16


def pack_kernel(gate_ref, up_ref, down_ref, out_ref):
    units, width = gate_ref.shape
    spare = jnp.zeros((LIFT_ROWS - 2 * units, width), out_ref.dtype)
    out_ref[...] = jnp.concatenate([gate_ref[...], up_ref[...], spare, down_ref[...]], axis=0)


def pack_weights(gate_across, up_across, down):
    units, width = down.shape
    depth = LIFT_ROWS + units
    return pl.pallas_call(
        pack_kernel,
        out_shape=jax.ShapeDtypeStruct((depth, width), down.dtype),
        compiler_params=pltpu.CompilerParams(vmem_limit_bytes=56 * 1024 * 1024),
        cost_estimate=pl.CostEstimate(
            flops=0, bytes_accessed=4 * depth * width, transcendentals=0
        ),
    )(gate_across, up_across, down)


def chunk_turn(chunks, back):
    side = GROUP * chunks
    share = CAP // chunks
    row = lax.broadcasted_iota(jnp.int32, (side, side), 1 if back else 0)
    col = lax.broadcasted_iota(jnp.int32, (side, side), 0 if back else 1)
    block, rest = row // (chunks * share), row % (chunks * share)
    source = (rest // share) * GROUP + block * share + rest % share
    return (source == col).astype(jnp.bfloat16)


def store_chunks(rows_ref, out_ref):
    count, width = rows_ref.shape
    chunks = out_ref.shape[0] // count
    turn = chunk_turn(chunks, False)
    for first in range(0, count, GROUP):
        pieces = []
        for chunk in range(chunks):
            low, high = chunk * CHUNK, min((chunk + 1) * CHUNK, width)
            piece = rows_ref[first : first + GROUP, low:high]
            if high - low < CHUNK:
                fill = jnp.zeros((GROUP, CHUNK - (high - low)), piece.dtype)
                piece = jnp.concatenate([piece, fill], axis=1)
            pieces.append(piece)
        stacked = jnp.concatenate(pieces, axis=0).astype(jnp.bfloat16)
        out_ref[first * chunks : (first + GROUP) * chunks, :] = jnp.dot(
            turn, stacked, preferred_element_type=jnp.float32
        ).astype(out_ref.dtype)


def load_chunks(chunks_ref, count):
    chunks = chunks_ref.shape[0] // count
    turn = chunk_turn(chunks, True)
    rows = []
    for first in range(0, count, GROUP):
        stacked = jnp.dot(
            turn,
            chunks_ref[first * chunks : (first + GROUP) * chunks, :],
            preferred_element_type=jnp.float32,
        )
        rows.append(
            jnp.concatenate([stacked[i * GROUP : (i + 1) * GROUP] for i in range(chunks)], axis=1)
        )
    return jnp.concatenate(rows, axis=0)


def combine_kernel(combiner_ref, chunks_ref, out_ref):
    width = out_ref.shape[1]
    rows = load_chunks(chunks_ref, combiner_ref.shape[1])[:, :width].astype(jnp.bfloat16)
    out_ref[...] = jnp.dot(
        combiner_ref[...], rows, preferred_element_type=jnp.float32
    ).astype(out_ref.dtype)


def run_combine(combiner, chunk_rows, width):
    tokens, count = combiner.shape
    return pl.pallas_call(
        combine_kernel,
        out_shape=jax.ShapeDtypeStruct((tokens, width), jnp.bfloat16),
        compiler_params=pltpu.CompilerParams(vmem_limit_bytes=24 * 1024 * 1024),
        cost_estimate=pl.CostEstimate(
            flops=2 * tokens * count * width, bytes_accessed=4 * tokens * width, transcendentals=0
        ),
    )(combiner, chunk_rows)


def select_kernel(selector_ref, normed_ref, out_ref, rows_ref):
    rows_ref[...] = jnp.dot(
        selector_ref[...], normed_ref[...], preferred_element_type=jnp.float32
    )
    store_chunks(rows_ref, out_ref)


def run_select(selector, normed):
    count, depth = selector.shape
    width = normed.shape[1]
    chunks = -(-width // CHUNK)
    return pl.pallas_call(
        select_kernel,
        out_shape=jax.ShapeDtypeStruct((count * chunks, CHUNK), jnp.bfloat16),
        scratch_shapes=[pltpu.VMEM((count, width), jnp.float32)],
        compiler_params=pltpu.CompilerParams(vmem_limit_bytes=24 * 1024 * 1024),
        cost_estimate=pl.CostEstimate(
            flops=4 * count * depth * width, bytes_accessed=4 * count * width, transcendentals=0
        ),
    )(selector, normed)


def expert_kernel(chunks_ref, weight_ref, out_ref, total_ref, across_ref):
    step = pl.program_id(0)
    units = weight_ref.shape[1] - LIFT_ROWS
    cut = LIFT_ROWS // 32 * 16
    count, width = total_ref.shape
    chunks = chunks_ref.shape[0] // count

    @pl.when(step == 0)
    def _():
        total_ref[...] = jnp.zeros_like(total_ref)
        across = load_chunks(chunks_ref, count).T
        across_ref[...] = across[:width].astype(across_ref.dtype)

    rows_across = across_ref[...]
    both = jnp.concatenate(
        [
            jnp.dot(weight_ref[0, :cut, :], rows_across, preferred_element_type=jnp.float32),
            jnp.dot(
                weight_ref[0, cut:LIFT_ROWS, :], rows_across, preferred_element_type=jnp.float32
            ),
        ],
        axis=0,
    )
    gate = both[:units]
    lifted = both[units : 2 * units]
    hidden = gate * jax.nn.sigmoid(1.702 * gate) * (lifted + 1.0)
    total_ref[...] += jnp.dot(
        hidden.T.astype(jnp.bfloat16),
        weight_ref[0, LIFT_ROWS:, :],
        preferred_element_type=jnp.float32,
    )

    @pl.when(step == pl.num_programs(0) - 1)
    def _():
        store_chunks(total_ref, out_ref)


def run_expert(chunk_rows, weights):
    groups, depth, width = weights.shape
    chunks = -(-width // CHUNK)
    count = chunk_rows.shape[0] // chunks
    return pl.pallas_call(
        expert_kernel,
        grid=(groups,),
        in_specs=[
            pl.BlockSpec((count * chunks, CHUNK), lambda g: (0, 0)),
            pl.BlockSpec((1, depth, width), lambda g: (g, 0, 0)),
        ],
        out_specs=pl.BlockSpec((count * chunks, CHUNK), lambda g: (0, 0)),
        out_shape=jax.ShapeDtypeStruct((count * chunks, CHUNK), jnp.bfloat16),
        scratch_shapes=[
            pltpu.VMEM((count, width), jnp.float32),
            pltpu.VMEM((width, count), jnp.bfloat16),
        ],
        compiler_params=pltpu.CompilerParams(vmem_limit_bytes=40 * 1024 * 1024),
        cost_estimate=pl.CostEstimate(
            flops=2 * count * width * depth * groups,
            bytes_accessed=groups * depth * width * 2,
            transcendentals=count * depth * groups // 3,
        ),
    )(chunk_rows, weights)


def on_device(
    queries,
    keys_values,
    sinks,
    out_weight,
    hidden_in,
    norm_gain,
    expert_ids,
    expert_gates,
    gate_weight,
    up_weight,
    down_weight,
):
    seq_devices = lax.axis_size("seq")
    exp_devices = lax.axis_size("exp")
    block_rows = queries.shape[1]
    heads = sinks.shape[0]
    width = out_weight.shape[1]
    own_rows = hidden_in.shape[1]
    units = gate_weight.shape[2]
    seq_rank = lax.axis_index("seq")
    exp_rank = lax.axis_index("exp")
    run_rows = RUN * block_rows
    runs = seq_devices // RUN

    with jax.named_scope("gather_weights"):
        weights = lax.all_gather(
            pack_weights(gate_weight[0].T, up_weight[0].T, down_weight[0]),
            "exp",
            axis=0,
            tiled=False,
        )

    with jax.named_scope("gather_keys"):
        run_groups = [[r * RUN + i for i in range(RUN)] for r in range(runs)]
        copies = jnp.broadcast_to(keys_values, (RUN,) + keys_values.shape[1:])
        near = lax.all_to_all(
            copies, "seq", split_axis=0, concat_axis=0, tiled=True, axis_index_groups=run_groups
        )
        near = near.reshape(run_rows, 2 * HEAD)
        far = lax.ppermute(near, "seq", [(i, i + RUN) for i in range(seq_devices - RUN)])

    with jax.named_scope("attend"):
        grid = queries[0].reshape(block_rows, heads, HEAD)
        query_pos = seq_rank * block_rows + jnp.arange(block_rows, dtype=jnp.int32)
        first_near = (seq_rank // RUN) * run_rows
        offsets = jnp.arange(run_rows, dtype=jnp.int32)

        def score(keys, key_pos, keep):
            raw = (
                jnp.einsum("igd,jd->gij", grid, keys, preferred_element_type=jnp.float32) * 0.125
            )
            return jnp.where((key_pos[None, :] <= query_pos[:, None]) & keep, raw, -1e30)

        def part(rows, key_pos, keep):
            scores = score(rows[:, :HEAD], key_pos, keep)
            top = jnp.max(scores, axis=-1)
            numerators = jnp.exp(scores - top[..., None])
            weighted = jnp.einsum(
                "gij,jd->gid",
                numerators.astype(jnp.bfloat16),
                rows[:, HEAD:],
                preferred_element_type=jnp.float32,
            )
            return top, jnp.sum(numerators, axis=-1), weighted

        near_top, near_sum, near_mix = part(near, first_near + offsets, True)
        far_top, far_sum, far_mix = part(far, first_near - run_rows + offsets, seq_rank >= RUN)
        largest = jnp.maximum(jnp.maximum(near_top, far_top), sinks[:, None])
        near_scale = jnp.exp(near_top - largest)
        far_scale = jnp.exp(far_top - largest)
        totals = near_sum * near_scale + far_sum * far_scale + jnp.exp(sinks[:, None] - largest)
        weighted = near_mix * near_scale[..., None] + far_mix * far_scale[..., None]
        mixed = (weighted / totals[..., None]).astype(jnp.bfloat16)
        heads_out = mixed.transpose(1, 0, 2).reshape(block_rows, heads * HEAD)

    with jax.named_scope("project"):
        head_term = jnp.dot(heads_out, out_weight, preferred_element_type=jnp.float32)
        chips = exp_devices // CORES
        core = exp_rank % CORES
        head_parts = head_term.reshape(chips, CORES, own_rows, width)
        given = lax.dynamic_index_in_dim(head_parts, 1 - core, 1, keepdims=False)
        kept = lax.dynamic_index_in_dim(head_parts, core, 1, keepdims=False)
        taken = lax.ppermute(
            given.astype(jnp.bfloat16), "exp", [(i, i ^ 1) for i in range(exp_devices)]
        )
        pair = (kept + taken.astype(jnp.float32)).astype(jnp.bfloat16)
        columns = [[CORES * i + c for i in range(chips)] for c in range(CORES)]
        own_parts = lax.all_to_all(
            pair, "exp", split_axis=0, concat_axis=0, tiled=True, axis_index_groups=columns
        )
        attention = jnp.sum(own_parts.astype(jnp.float32), axis=0)
        residual = (hidden_in[0].astype(jnp.float32) + attention).astype(jnp.bfloat16)

    with jax.named_scope("norm"):
        stream = residual.astype(jnp.float32)
        mean_square = jnp.mean(stream * stream, axis=-1, keepdims=True)
        normed_own = (stream * lax.rsqrt(mean_square + 1e-05) * norm_gain).astype(jnp.bfloat16)
        normed = lax.all_gather(normed_own, "exp", axis=0, tiled=True)

    with jax.named_scope("route"):
        chosen = expert_ids[0]
        share = CAP // exp_devices
        hits = (chosen[:, :, None] == jnp.arange(seq_devices, dtype=jnp.int32)).astype(jnp.float32)
        token_hits = jnp.sum(hits, axis=1)
        earlier = (
            jnp.arange(block_rows)[:, None] > jnp.arange(block_rows)[None, :]
        ).astype(jnp.float32)
        slots = jnp.dot(earlier, token_hits)
        named = token_hits[:, :, None] > 0
        wanted = (exp_rank * share + jnp.arange(share, dtype=jnp.int32)).astype(jnp.float32)
        picks = named & (slots[:, :, None] == wanted)
        selector = picks.astype(jnp.bfloat16).reshape(block_rows, seq_devices * share).T
        factor = jnp.einsum("tke,tk->te", hits, expert_gates[0].astype(jnp.float32))
        combiner = jnp.where(picks, factor[:, :, None], 0.0).astype(jnp.bfloat16)
        chunks = -(-width // CHUNK)
        combiner = combiner.reshape(block_rows, seq_devices * share)

    with jax.named_scope("dispatch"):
        outgoing = run_select(selector, normed).reshape(seq_devices, chunks * share, CHUNK)
        arrived = lax.all_to_all(outgoing, "seq", split_axis=0, concat_axis=0, tiled=True)

    with jax.named_scope("experts"):
        done = run_expert(arrived.reshape(seq_devices * chunks * share, CHUNK), weights)

    with jax.named_scope("combine"):
        returned = lax.all_to_all(
            done.reshape(seq_devices, chunks * share, CHUNK),
            "seq",
            split_axis=0,
            concat_axis=0,
            tiled=True,
        )
        term = run_combine(
            combiner, returned.reshape(seq_devices * chunks * share, CHUNK), width
        )
        terms = lax.all_to_all(
            term.reshape(exp_devices, own_rows, width),
            "exp",
            split_axis=0,
            concat_axis=0,
            tiled=True,
        )
        expert_sum = jnp.sum(terms.astype(jnp.float32), axis=0)
        layer_out = (residual.astype(jnp.float32) + expert_sum).astype(jnp.bfloat16)
    return layer_out[None]


def solution(mesh):
    placed = (
        P("batch", "seq", "exp"),
        P("batch", "seq", "exp"),
        P("exp"),
        P("exp", None),
        P("batch", ("seq", "exp"), None),
        P(),
        P("batch", "seq", None),
        P("batch", "seq", None),
        P("seq", None, "exp"),
        P("seq", None, "exp"),
        P("seq", "exp", None),
    )
    return jax.shard_map(
        on_device,
        mesh=mesh,
        in_specs=placed,
        out_specs=P("batch", ("seq", "exp"), None),
        check_vma=False,
    )
```

```python
import jax
import jax.numpy as jnp
from jax import lax
from jax.experimental import pallas as pl
from jax.experimental.pallas import tpu as pltpu
from jax.sharding import PartitionSpec as P

HEAD = 64
TILE = 16
CHUNK = 384
CAP = 24
GROUP = 24
CORES = 2
RUN = 16


def pack_kernel(gate_ref, up_ref, down_ref, out_ref):
    out_ref[...] = jnp.concatenate([gate_ref[...], up_ref[...], down_ref[...]], axis=0)


def pack_weights(gate_across, up_across, down):
    units, width = down.shape
    depth = 3 * units
    return pl.pallas_call(
        pack_kernel,
        out_shape=jax.ShapeDtypeStruct((depth, width), down.dtype),
        compiler_params=pltpu.CompilerParams(vmem_limit_bytes=56 * 1024 * 1024),
        cost_estimate=pl.CostEstimate(
            flops=0, bytes_accessed=4 * depth * width, transcendentals=0
        ),
    )(gate_across, up_across, down)


def chunk_turn(chunks, back):
    side = GROUP * chunks
    share = CAP // chunks
    row = lax.broadcasted_iota(jnp.int32, (side, side), 1 if back else 0)
    col = lax.broadcasted_iota(jnp.int32, (side, side), 0 if back else 1)
    block, rest = row // (chunks * share), row % (chunks * share)
    source = (rest // share) * GROUP + block * share + rest % share
    return (source == col).astype(jnp.bfloat16)


def store_chunks(rows_ref, out_ref):
    count, width = rows_ref.shape
    chunks = out_ref.shape[0] // count
    turn = chunk_turn(chunks, False)
    for first in range(0, count, GROUP):
        pieces = []
        for chunk in range(chunks):
            low, high = chunk * CHUNK, min((chunk + 1) * CHUNK, width)
            piece = rows_ref[first : first + GROUP, low:high]
            if high - low < CHUNK:
                fill = jnp.zeros((GROUP, CHUNK - (high - low)), piece.dtype)
                piece = jnp.concatenate([piece, fill], axis=1)
            pieces.append(piece)
        stacked = jnp.concatenate(pieces, axis=0).astype(jnp.bfloat16)
        out_ref[first * chunks : (first + GROUP) * chunks, :] = jnp.dot(
            turn, stacked, preferred_element_type=jnp.float32
        ).astype(out_ref.dtype)


def load_chunks(chunks_ref, count):
    chunks = chunks_ref.shape[0] // count
    turn = chunk_turn(chunks, True)
    rows = []
    for first in range(0, count, GROUP):
        stacked = jnp.dot(
            turn,
            chunks_ref[first * chunks : (first + GROUP) * chunks, :],
            preferred_element_type=jnp.float32,
        )
        rows.append(
            jnp.concatenate([stacked[i * GROUP : (i + 1) * GROUP] for i in range(chunks)], axis=1)
        )
    return jnp.concatenate(rows, axis=0)


def combine_kernel(combiner_ref, chunks_ref, out_ref):
    width = out_ref.shape[1]
    rows = load_chunks(chunks_ref, combiner_ref.shape[1])[:, :width].astype(jnp.bfloat16)
    out_ref[...] = jnp.dot(
        combiner_ref[...], rows, preferred_element_type=jnp.float32
    ).astype(out_ref.dtype)


def run_combine(combiner, chunk_rows, width):
    tokens, count = combiner.shape
    return pl.pallas_call(
        combine_kernel,
        out_shape=jax.ShapeDtypeStruct((tokens, width), jnp.bfloat16),
        compiler_params=pltpu.CompilerParams(vmem_limit_bytes=24 * 1024 * 1024),
        cost_estimate=pl.CostEstimate(
            flops=2 * tokens * count * width, bytes_accessed=4 * tokens * width, transcendentals=0
        ),
    )(combiner, chunk_rows)


def select_kernel(selector_ref, normed_ref, out_ref, rows_ref):
    rows_ref[...] = jnp.dot(
        selector_ref[...], normed_ref[...], preferred_element_type=jnp.float32
    )
    store_chunks(rows_ref, out_ref)


def run_select(selector, normed):
    count, depth = selector.shape
    width = normed.shape[1]
    chunks = -(-width // CHUNK)
    return pl.pallas_call(
        select_kernel,
        out_shape=jax.ShapeDtypeStruct((count * chunks, CHUNK), jnp.bfloat16),
        scratch_shapes=[pltpu.VMEM((count, width), jnp.float32)],
        compiler_params=pltpu.CompilerParams(vmem_limit_bytes=24 * 1024 * 1024),
        cost_estimate=pl.CostEstimate(
            flops=4 * count * depth * width, bytes_accessed=4 * count * width, transcendentals=0
        ),
    )(selector, normed)


def group_term(weight_ref, rows_across):
    units = weight_ref.shape[0] // 3
    count = rows_across.shape[1]
    lift_rows = -(-2 * units // TILE) * TILE
    down_from = 2 * units // TILE * TILE
    cut = lift_rows // (2 * TILE) * TILE
    both = jnp.concatenate(
        [
            jnp.dot(weight_ref[:cut, :], rows_across, preferred_element_type=jnp.float32),
            jnp.dot(
                weight_ref[cut:lift_rows, :], rows_across, preferred_element_type=jnp.float32
            ),
        ],
        axis=0,
    )
    gate = both[:units]
    lifted = both[units : 2 * units]
    hidden = gate * jax.nn.sigmoid(1.702 * gate) * (lifted + 1.0)
    lead = jnp.zeros((2 * units - down_from, count), jnp.float32)
    hidden = jnp.concatenate([lead, hidden], axis=0)
    return jnp.dot(
        hidden.T.astype(jnp.bfloat16),
        weight_ref[down_from:, :],
        preferred_element_type=jnp.float32,
    )


def peer_kernel(chunks_ref, peer_ref, total_ref, held_ref, sem):
    count, width = total_ref.shape
    copy = pltpu.make_async_copy(peer_ref, held_ref, sem)
    copy.start()
    rows_across = load_chunks(chunks_ref, count).T[:width].astype(jnp.bfloat16)
    copy.wait()
    total_ref[...] = group_term(held_ref, rows_across)


def run_peer(chunk_rows, peer):
    depth, width = peer.shape
    count = chunk_rows.shape[0] // -(-width // CHUNK)
    return pl.pallas_call(
        peer_kernel,
        in_specs=[
            pl.BlockSpec(memory_space=pltpu.VMEM),
            pl.BlockSpec(memory_space=pl.ANY),
        ],
        out_specs=pl.BlockSpec(memory_space=pltpu.VMEM),
        out_shape=jax.ShapeDtypeStruct((count, width), jnp.float32),
        scratch_shapes=[
            pltpu.VMEM((depth, width), jnp.bfloat16),
            pltpu.SemaphoreType.DMA,
        ],
        compiler_params=pltpu.CompilerParams(vmem_limit_bytes=24 * 1024 * 1024),
        cost_estimate=pl.CostEstimate(
            flops=2 * count * width * depth,
            bytes_accessed=2 * depth * width,
            transcendentals=count * depth // 3,
        ),
    )(chunk_rows, peer)


def expert_kernel(
    chunks_ref, start_ref, weight_ref, out_ref, held_ref, total_ref, ready_ref, sems, out_sems
):
    groups = weight_ref.shape[0]
    others = held_ref.shape[0]
    count, width = total_ref.shape
    rank = lax.axis_index("exp")
    first = rank // CORES * CORES + CORES

    def fetch(i):
        group = lax.rem(first + i, groups) if i < groups - CORES else rank
        return pltpu.make_async_copy(weight_ref.at[group], held_ref.at[i], sems.at[i])

    for i in range(others):
        fetch(i).start()
    total_ref[...] = start_ref[...]
    rows_across = load_chunks(chunks_ref, count).T[:width].astype(jnp.bfloat16)
    for i in range(others):
        fetch(i).wait()
        total_ref[...] += group_term(held_ref.at[i], rows_across)
    store_chunks(total_ref, ready_ref)
    copy = pltpu.make_async_copy(ready_ref, out_ref, out_sems)
    copy.start()
    copy.wait()


def run_expert(chunk_rows, start, weights):
    groups, depth, width = weights.shape
    count = start.shape[0]
    others = groups - 1
    return pl.pallas_call(
        expert_kernel,
        in_specs=[
            pl.BlockSpec(memory_space=pltpu.VMEM),
            pl.BlockSpec(memory_space=pltpu.VMEM),
            pl.BlockSpec(memory_space=pl.ANY),
        ],
        out_specs=pl.BlockSpec(memory_space=pltpu.HBM),
        out_shape=jax.ShapeDtypeStruct(chunk_rows.shape, jnp.bfloat16),
        scratch_shapes=[
            pltpu.VMEM((others, depth, width), jnp.bfloat16),
            pltpu.VMEM((count, width), jnp.float32),
            pltpu.VMEM(chunk_rows.shape, jnp.bfloat16),
            pltpu.SemaphoreType.DMA((others,)),
            pltpu.SemaphoreType.DMA,
        ],
        compiler_params=pltpu.CompilerParams(vmem_limit_bytes=44 * 1024 * 1024),
        cost_estimate=pl.CostEstimate(
            flops=2 * count * width * depth * others,
            bytes_accessed=others * depth * width * 2,
            transcendentals=count * depth * others // 3,
        ),
    )(chunk_rows, start, weights)


def on_device(
    queries,
    keys_values,
    sinks,
    out_weight,
    hidden_in,
    norm_gain,
    expert_ids,
    expert_gates,
    gate_weight,
    up_weight,
    down_weight,
):
    seq_devices = lax.axis_size("seq")
    exp_devices = lax.axis_size("exp")
    block_rows = queries.shape[1]
    heads = sinks.shape[0]
    width = out_weight.shape[1]
    own_rows = hidden_in.shape[1]
    units = gate_weight.shape[2]
    seq_rank = lax.axis_index("seq")
    exp_rank = lax.axis_index("exp")
    run_rows = RUN * block_rows
    runs = seq_devices // RUN

    with jax.named_scope("gather_weights"):
        weights_own = pack_weights(gate_weight[0].T, up_weight[0].T, down_weight[0])
        weights = lax.all_gather(weights_own, "exp", axis=0, tiled=False)
        swap = [(i, i ^ 1) for i in range(exp_devices)]
        weights_peer = lax.ppermute(weights_own, "exp", swap)

    with jax.named_scope("gather_keys"):
        run_groups = [[r * RUN + i for i in range(RUN)] for r in range(runs)]
        copies = jnp.broadcast_to(keys_values, (RUN,) + keys_values.shape[1:])
        near = lax.all_to_all(
            copies, "seq", split_axis=0, concat_axis=0, tiled=True, axis_index_groups=run_groups
        )
        near = near.reshape(run_rows, 2 * HEAD)
        to_far = [(i, i + RUN) for i in range(seq_devices - RUN)]
        to_near = [(i + RUN, i) for i in range(seq_devices - RUN)]
        guests = lax.ppermute(queries[0], "seq", to_near)

    with jax.named_scope("route"):
        chips = exp_devices // CORES
        core = exp_rank % CORES
        chosen = expert_ids[0]
        share = CAP // exp_devices
        hits = (chosen[:, :, None] == jnp.arange(seq_devices, dtype=jnp.int32)).astype(jnp.float32)
        token_hits = jnp.sum(hits, axis=1)
        earlier = (
            jnp.arange(block_rows)[:, None] > jnp.arange(block_rows)[None, :]
        ).astype(jnp.float32)
        slots = jnp.dot(earlier, token_hits)
        named = token_hits[:, :, None] > 0
        wanted = (exp_rank * share + jnp.arange(share, dtype=jnp.int32)).astype(jnp.float32)
        picks = named & (slots[:, :, None] == wanted)
        selector = picks.astype(jnp.bfloat16).reshape(
            chips, CORES, own_rows, seq_devices * share
        )
        selector = selector.transpose(3, 1, 0, 2).reshape(seq_devices * share, block_rows)
        factor = jnp.einsum("tke,tk->te", hits, expert_gates[0].astype(jnp.float32))
        combiner = jnp.where(picks, factor[:, :, None], 0.0).astype(jnp.bfloat16)
        chunks = -(-width // CHUNK)
        combiner = combiner.reshape(block_rows, seq_devices * share)
        selector, combiner, near = lax.optimization_barrier((selector, combiner, near))

    with jax.named_scope("attend"):
        grid = jnp.concatenate([queries[0], guests], axis=0)
        grid = grid.reshape(2 * block_rows, heads, HEAD)
        own_pos = (seq_rank % RUN) * block_rows + jnp.arange(block_rows, dtype=jnp.int32)
        query_pos = jnp.concatenate([own_pos, jnp.full((block_rows,), run_rows, jnp.int32)])
        key_pos = jnp.arange(run_rows, dtype=jnp.int32)
        scores = (
            jnp.einsum("igd,jd->gij", grid, near[:, :HEAD], preferred_element_type=jnp.float32)
            * 0.125
        )
        scores = jnp.where(key_pos[None, :] <= query_pos[:, None], scores, -1e30)
        top = jnp.max(scores, axis=-1)
        numerators = jnp.exp(scores - top[..., None])
        sums = jnp.sum(numerators, axis=-1)
        weighted = jnp.einsum(
            "gij,jd->gid",
            numerators.astype(jnp.bfloat16),
            near[:, HEAD:],
            preferred_element_type=jnp.float32,
        )
        guest_stats = jnp.stack([top[:, block_rows:], sums[:, block_rows:]])
        guest_mix = weighted[:, block_rows:].astype(jnp.bfloat16)
        far_stats = lax.ppermute(guest_stats, "seq", to_far)
        far_mix = lax.ppermute(guest_mix, "seq", to_far)
        top, sums, weighted = top[:, :block_rows], sums[:, :block_rows], weighted[:, :block_rows]
        far_top = jnp.where(seq_rank >= RUN, far_stats[0], -1e30)
        largest = jnp.maximum(jnp.maximum(top, far_top), sinks[:, None])
        near_scale = jnp.exp(top - largest)
        far_scale = jnp.exp(far_top - largest)
        totals = (
            sums * near_scale + far_stats[1] * far_scale + jnp.exp(sinks[:, None] - largest)
        )
        weighted = (
            weighted * near_scale[..., None]
            + far_mix.astype(jnp.float32) * far_scale[..., None]
        )
        mixed = (weighted / totals[..., None]).astype(jnp.bfloat16)
        heads_out = mixed.transpose(1, 0, 2).reshape(block_rows, heads * HEAD)

    with jax.named_scope("project"):
        head_term = jnp.dot(heads_out, out_weight, preferred_element_type=jnp.float32)
        head_parts = head_term.reshape(chips, CORES, own_rows, width)
        given = lax.dynamic_index_in_dim(head_parts, 1 - core, 1, keepdims=False)
        kept = lax.dynamic_index_in_dim(head_parts, core, 1, keepdims=False)
        taken = lax.ppermute(given.astype(jnp.bfloat16), "exp", swap)
        pair = (kept + taken.astype(jnp.float32)).astype(jnp.bfloat16)
        columns = [[CORES * i + c for i in range(chips)] for c in range(CORES)]
        own_parts = lax.all_to_all(
            pair, "exp", split_axis=0, concat_axis=0, tiled=True, axis_index_groups=columns
        )
        attention = jnp.sum(own_parts.astype(jnp.float32), axis=0)
        residual = (hidden_in[0].astype(jnp.float32) + attention).astype(jnp.bfloat16)

    with jax.named_scope("norm"):
        stream = residual.astype(jnp.float32)
        mean_square = jnp.mean(stream * stream, axis=-1, keepdims=True)
        normed_own = (stream * lax.rsqrt(mean_square + 1e-05) * norm_gain).astype(jnp.bfloat16)
        normed_own, weights_peer = lax.optimization_barrier((normed_own, weights_peer))
        normed = lax.all_gather(
            normed_own, "exp", axis=0, tiled=True, axis_index_groups=columns
        )
        cores = [[CORES * i + c for c in range(CORES)] for i in range(chips)]
        normed = lax.all_gather(normed, "exp", axis=0, tiled=True, axis_index_groups=cores)

    with jax.named_scope("dispatch"):
        outgoing = run_select(selector, normed).reshape(seq_devices, chunks * share, CHUNK)
        arrived = lax.all_to_all(outgoing, "seq", split_axis=0, concat_axis=0, tiled=True)

    with jax.named_scope("experts"):
        chunk_rows = arrived.reshape(seq_devices * chunks * share, CHUNK)
        start = run_peer(chunk_rows, weights_peer)
        done = run_expert(chunk_rows, start, weights)

    with jax.named_scope("combine"):
        returned = lax.all_to_all(
            done.reshape(seq_devices, chunks * share, CHUNK),
            "seq",
            split_axis=0,
            concat_axis=0,
            tiled=True,
        )
        term = run_combine(
            combiner, returned.reshape(seq_devices * chunks * share, CHUNK), width
        )
        terms = lax.all_to_all(
            term.reshape(exp_devices, own_rows, width),
            "exp",
            split_axis=0,
            concat_axis=0,
            tiled=True,
        )
        expert_sum = jnp.sum(terms.astype(jnp.float32), axis=0)
        layer_out = (residual.astype(jnp.float32) + expert_sum).astype(jnp.bfloat16)
    return layer_out[None]


def solution(mesh):
    placed = (
        P("batch", "seq", "exp"),
        P("batch", "seq", "exp"),
        P("exp"),
        P("exp", None),
        P("batch", ("seq", "exp"), None),
        P(),
        P("batch", "seq", None),
        P("batch", "seq", None),
        P("seq", None, "exp"),
        P("seq", None, "exp"),
        P("seq", "exp", None),
    )
    return jax.shard_map(
        on_device,
        mesh=mesh,
        in_specs=placed,
        out_specs=P("batch", ("seq", "exp"), None),
        check_vma=False,
    )
```

```python
import jax
import jax.numpy as jnp
from jax import lax
from jax.experimental import pallas as pl
from jax.experimental.pallas import tpu as pltpu
from jax.sharding import PartitionSpec as P

HEAD = 64
TILE = 16
LANES = 128
CHUNK = 384
CAP = 24
GROUP = 24
CORES = 2
RUN = 16


def pack_kernel(gate_ref, up_ref, down_ref, out_ref):
    half = up_ref.shape[0] // 2
    up = up_ref[...]
    left = jnp.concatenate([gate_ref[...], up[:half]], axis=0)
    right = jnp.concatenate([up[half:], down_ref[...]], axis=0)
    out_ref[...] = jnp.concatenate([left, right], axis=1)


def pack_weights(gate_across, up_across, down):
    units, width = down.shape
    depth = 3 * units
    return pl.pallas_call(
        pack_kernel,
        out_shape=jax.ShapeDtypeStruct((depth // 2, 2 * width), down.dtype),
        compiler_params=pltpu.CompilerParams(vmem_limit_bytes=56 * 1024 * 1024),
        cost_estimate=pl.CostEstimate(
            flops=0, bytes_accessed=4 * depth * width, transcendentals=0
        ),
    )(gate_across, up_across, down)


def chunk_turn(chunks, back):
    side = GROUP * chunks
    share = CAP // chunks
    row = lax.broadcasted_iota(jnp.int32, (side, side), 1 if back else 0)
    col = lax.broadcasted_iota(jnp.int32, (side, side), 0 if back else 1)
    block, rest = row // (chunks * share), row % (chunks * share)
    source = (rest // share) * GROUP + block * share + rest % share
    return (source == col).astype(jnp.bfloat16)


def store_chunks(rows_ref, out_ref):
    count, width = rows_ref.shape
    chunks = out_ref.shape[0] // count
    turn = chunk_turn(chunks, False)
    for first in range(0, count, GROUP):
        pieces = []
        for chunk in range(chunks):
            low, high = chunk * CHUNK, min((chunk + 1) * CHUNK, width)
            piece = rows_ref[first : first + GROUP, low:high]
            if high - low < CHUNK:
                fill = jnp.zeros((GROUP, CHUNK - (high - low)), piece.dtype)
                piece = jnp.concatenate([piece, fill], axis=1)
            pieces.append(piece)
        stacked = jnp.concatenate(pieces, axis=0).astype(jnp.bfloat16)
        out_ref[first * chunks : (first + GROUP) * chunks, :] = jnp.dot(
            turn, stacked, preferred_element_type=jnp.float32
        ).astype(out_ref.dtype)


def load_chunks(chunks_ref, count):
    chunks = chunks_ref.shape[0] // count
    turn = chunk_turn(chunks, True)
    rows = []
    for first in range(0, count, GROUP):
        stacked = jnp.dot(
            turn,
            chunks_ref[first * chunks : (first + GROUP) * chunks, :],
            preferred_element_type=jnp.float32,
        )
        rows.append(
            jnp.concatenate([stacked[i * GROUP : (i + 1) * GROUP] for i in range(chunks)], axis=1)
        )
    return jnp.concatenate(rows, axis=0)


def combine_kernel(combiner_ref, chunks_ref, out_ref):
    width = out_ref.shape[1]
    rows = load_chunks(chunks_ref, combiner_ref.shape[1])[:, :width].astype(jnp.bfloat16)
    out_ref[...] = jnp.dot(
        combiner_ref[...], rows, preferred_element_type=jnp.float32
    ).astype(out_ref.dtype)


def run_combine(combiner, chunk_rows, width):
    tokens, count = combiner.shape
    return pl.pallas_call(
        combine_kernel,
        out_shape=jax.ShapeDtypeStruct((tokens, width), jnp.bfloat16),
        compiler_params=pltpu.CompilerParams(vmem_limit_bytes=24 * 1024 * 1024),
        cost_estimate=pl.CostEstimate(
            flops=2 * tokens * count * width, bytes_accessed=4 * tokens * width, transcendentals=0
        ),
    )(combiner, chunk_rows)


def select_kernel(selector_ref, normed_ref, out_ref, rows_ref):
    rows_ref[...] = jnp.dot(
        selector_ref[...], normed_ref[...], preferred_element_type=jnp.float32
    )
    store_chunks(rows_ref, out_ref)


def run_select(selector, normed):
    count, depth = selector.shape
    width = normed.shape[1]
    chunks = -(-width // CHUNK)
    return pl.pallas_call(
        select_kernel,
        out_shape=jax.ShapeDtypeStruct((count * chunks, CHUNK), jnp.bfloat16),
        scratch_shapes=[pltpu.VMEM((count, width), jnp.float32)],
        compiler_params=pltpu.CompilerParams(vmem_limit_bytes=24 * 1024 * 1024),
        cost_estimate=pl.CostEstimate(
            flops=4 * count * depth * width, bytes_accessed=4 * count * width, transcendentals=0
        ),
    )(selector, normed)


def pad_across(rows_across):
    width, count = rows_across.shape
    spare = jnp.zeros((-width % LANES, count), rows_across.dtype)
    return (
        jnp.concatenate([rows_across, spare], axis=0),
        jnp.concatenate([spare, rows_across], axis=0),
    )


def group_term(weight_ref, across):
    span, count = across[0].shape
    units = weight_ref.shape[0] * 2 // 3
    half = units // 2
    low = weight_ref.shape[1] - span
    up_rows = -(-half // TILE) * TILE
    down_from = half // TILE * TILE
    cut = units // TILE * TILE
    left = jnp.concatenate(
        [
            jnp.dot(weight_ref[:cut, :span], across[0], preferred_element_type=jnp.float32),
            jnp.dot(weight_ref[cut:, :span], across[0], preferred_element_type=jnp.float32),
        ],
        axis=0,
    )
    right = jnp.dot(weight_ref[:up_rows, low:], across[1], preferred_element_type=jnp.float32)
    gate = left[:units]
    lifted = jnp.concatenate([left[units:], right[:half]], axis=0)
    hidden = gate * jax.nn.sigmoid(1.702 * gate) * (lifted + 1.0)
    lead = jnp.zeros((half - down_from, count), jnp.float32)
    return jnp.dot(
        jnp.concatenate([lead, hidden], axis=0).T.astype(jnp.bfloat16),
        weight_ref[down_from:, low:],
        preferred_element_type=jnp.float32,
    )


def peer_kernel(chunks_ref, peer_ref, total_ref, held_ref, sem):
    count, width = total_ref.shape
    copy = pltpu.make_async_copy(peer_ref, held_ref, sem)
    copy.start()
    rows_across = load_chunks(chunks_ref, count).T[:width].astype(jnp.bfloat16)
    across = pad_across(rows_across)
    copy.wait()
    term = group_term(held_ref, across)
    total_ref[...] = term[:, term.shape[1] - width :]


def run_peer(chunk_rows, peer):
    depth, width = peer.shape[0] * 2, peer.shape[1] // 2
    count = chunk_rows.shape[0] // -(-width // CHUNK)
    return pl.pallas_call(
        peer_kernel,
        in_specs=[
            pl.BlockSpec(memory_space=pltpu.VMEM),
            pl.BlockSpec(memory_space=pl.ANY),
        ],
        out_specs=pl.BlockSpec(memory_space=pltpu.VMEM),
        out_shape=jax.ShapeDtypeStruct((count, width), jnp.float32),
        scratch_shapes=[
            pltpu.VMEM(peer.shape, jnp.bfloat16),
            pltpu.SemaphoreType.DMA,
        ],
        compiler_params=pltpu.CompilerParams(vmem_limit_bytes=24 * 1024 * 1024),
        cost_estimate=pl.CostEstimate(
            flops=2 * count * width * depth,
            bytes_accessed=2 * depth * width,
            transcendentals=count * depth // 3,
        ),
    )(chunk_rows, peer)


def expert_kernel(
    chunks_ref, start_ref, weight_ref, out_ref, held_ref, total_ref, wide_ref, sems
):
    groups = weight_ref.shape[0]
    others = held_ref.shape[0]
    count, width = total_ref.shape
    rank = lax.axis_index("exp")
    first = rank // CORES * CORES + CORES

    def fetch(i):
        group = lax.rem(first + i, groups) if i < groups - CORES else rank
        return pltpu.make_async_copy(weight_ref.at[group], held_ref.at[i], sems.at[i])

    for i in range(others):
        fetch(i).start()
    rows_across = load_chunks(chunks_ref, count).T[:width].astype(jnp.bfloat16)
    across = pad_across(rows_across)
    for i in range(others):
        fetch(i).wait()
        term = group_term(held_ref.at[i], across)
        if i == 0:
            wide_ref[...] = term
        else:
            wide_ref[...] += term
    total_ref[...] = start_ref[...] + wide_ref[:, wide_ref.shape[1] - width :]
    store_chunks(total_ref, out_ref)


def run_expert(chunk_rows, start, weights):
    groups, depth, _ = weights.shape
    count, width = start.shape
    others = groups - 1
    span = -(-width // LANES) * LANES
    return pl.pallas_call(
        expert_kernel,
        in_specs=[
            pl.BlockSpec(memory_space=pltpu.VMEM),
            pl.BlockSpec(memory_space=pltpu.VMEM),
            pl.BlockSpec(memory_space=pl.ANY),
        ],
        out_specs=pl.BlockSpec(memory_space=pltpu.VMEM),
        out_shape=jax.ShapeDtypeStruct(chunk_rows.shape, jnp.bfloat16),
        scratch_shapes=[
            pltpu.VMEM((others,) + weights.shape[1:], jnp.bfloat16),
            pltpu.VMEM((count, width), jnp.float32),
            pltpu.VMEM((count, span), jnp.float32),
            pltpu.SemaphoreType.DMA((others,)),
        ],
        compiler_params=pltpu.CompilerParams(vmem_limit_bytes=44 * 1024 * 1024),
        cost_estimate=pl.CostEstimate(
            flops=4 * count * width * depth * others,
            bytes_accessed=others * depth * width * 4,
            transcendentals=count * depth * others // 2,
        ),
    )(chunk_rows, start, weights)


def on_device(
    queries,
    keys_values,
    sinks,
    out_weight,
    hidden_in,
    norm_gain,
    expert_ids,
    expert_gates,
    gate_weight,
    up_weight,
    down_weight,
):
    seq_devices = lax.axis_size("seq")
    exp_devices = lax.axis_size("exp")
    block_rows = queries.shape[1]
    heads = sinks.shape[0]
    width = out_weight.shape[1]
    own_rows = hidden_in.shape[1]
    units = gate_weight.shape[2]
    seq_rank = lax.axis_index("seq")
    exp_rank = lax.axis_index("exp")
    run_rows = RUN * block_rows
    runs = seq_devices // RUN

    with jax.named_scope("gather_weights"):
        weights_own = pack_weights(gate_weight[0].T, up_weight[0].T, down_weight[0])
        weights = lax.all_gather(weights_own, "exp", axis=0, tiled=False)
        swap = [(i, i ^ 1) for i in range(exp_devices)]
        weights_peer = lax.ppermute(weights_own, "exp", swap)

    with jax.named_scope("gather_keys"):
        run_groups = [[r * RUN + i for i in range(RUN)] for r in range(runs)]
        copies = jnp.broadcast_to(keys_values, (RUN,) + keys_values.shape[1:])
        near = lax.all_to_all(
            copies, "seq", split_axis=0, concat_axis=0, tiled=True, axis_index_groups=run_groups
        )
        near = near.reshape(run_rows, 2 * HEAD)
        to_far = [(i, i + RUN) for i in range(seq_devices - RUN)]
        to_near = [(i + RUN, i) for i in range(seq_devices - RUN)]
        guests = lax.ppermute(queries[0], "seq", to_near)

    with jax.named_scope("route"):
        chips = exp_devices // CORES
        core = exp_rank % CORES
        chosen = expert_ids[0]
        share = CAP // exp_devices
        hits = (chosen[:, :, None] == jnp.arange(seq_devices, dtype=jnp.int32)).astype(jnp.float32)
        token_hits = jnp.sum(hits, axis=1)
        earlier = (
            jnp.arange(block_rows)[:, None] > jnp.arange(block_rows)[None, :]
        ).astype(jnp.float32)
        slots = jnp.dot(earlier, token_hits)
        named = token_hits[:, :, None] > 0
        wanted = (exp_rank * share + jnp.arange(share, dtype=jnp.int32)).astype(jnp.float32)
        picks = named & (slots[:, :, None] == wanted)
        selector = picks.astype(jnp.bfloat16).reshape(
            chips, CORES, own_rows, seq_devices * share
        )
        selector = selector.transpose(3, 1, 0, 2).reshape(seq_devices * share, block_rows)
        factor = jnp.einsum("tke,tk->te", hits, expert_gates[0].astype(jnp.float32))
        combiner = jnp.where(picks, factor[:, :, None], 0.0).astype(jnp.bfloat16)
        chunks = -(-width // CHUNK)
        combiner = combiner.reshape(block_rows, seq_devices * share)
        selector, combiner, near = lax.optimization_barrier((selector, combiner, near))

    with jax.named_scope("attend"):
        own_pos = (seq_rank % RUN) * block_rows + jnp.arange(block_rows, dtype=jnp.int32)
        key_pos = jnp.arange(run_rows, dtype=jnp.int32)

        def attend(rows, allowed):
            scores = (
                jnp.einsum(
                    "igd,jd->gij",
                    rows.reshape(block_rows, heads, HEAD),
                    near[:, :HEAD],
                    preferred_element_type=jnp.float32,
                )
                * 0.125
            )
            if allowed is not None:
                scores = jnp.where(allowed, scores, -1e30)
            top = jnp.max(scores, axis=-1)
            numerators = jnp.exp(scores - top[..., None])
            mix = jnp.einsum(
                "gij,jd->gid",
                numerators.astype(jnp.bfloat16),
                near[:, HEAD:],
                preferred_element_type=jnp.float32,
            )
            return top, jnp.sum(numerators, axis=-1), mix

        guest_top, guest_sum, guest_mix = attend(guests, None)
        far_mix = lax.ppermute(guest_mix.astype(jnp.bfloat16), "seq", to_far)
        far_stats = lax.ppermute(jnp.stack([guest_top, guest_sum]), "seq", to_far)
        top, sums, weighted = attend(queries[0], key_pos[None, :] <= own_pos[:, None])
        far_top = jnp.where(seq_rank >= RUN, far_stats[0], -1e30)
        largest = jnp.maximum(jnp.maximum(top, far_top), sinks[:, None])
        near_scale = jnp.exp(top - largest)
        far_scale = jnp.exp(far_top - largest)
        totals = (
            sums * near_scale + far_stats[1] * far_scale + jnp.exp(sinks[:, None] - largest)
        )
        weighted = (
            weighted * near_scale[..., None]
            + far_mix.astype(jnp.float32) * far_scale[..., None]
        )
        mixed = (weighted / totals[..., None]).astype(jnp.bfloat16)
        heads_out = mixed.transpose(1, 0, 2).reshape(block_rows, heads * HEAD)

    with jax.named_scope("project"):
        head_term = jnp.dot(heads_out, out_weight, preferred_element_type=jnp.float32)
        head_parts = head_term.reshape(chips, CORES, own_rows, width)
        given = lax.dynamic_index_in_dim(head_parts, 1 - core, 1, keepdims=False)
        kept = lax.dynamic_index_in_dim(head_parts, core, 1, keepdims=False)
        taken = lax.ppermute(given.astype(jnp.bfloat16), "exp", swap)
        pair = (kept + taken.astype(jnp.float32)).astype(jnp.bfloat16)
        columns = [[CORES * i + c for i in range(chips)] for c in range(CORES)]
        own_parts = lax.all_to_all(
            pair, "exp", split_axis=0, concat_axis=0, tiled=True, axis_index_groups=columns
        )
        attention = jnp.sum(own_parts.astype(jnp.float32), axis=0)
        residual = (hidden_in[0].astype(jnp.float32) + attention).astype(jnp.bfloat16)

    with jax.named_scope("norm"):
        stream = residual.astype(jnp.float32)
        mean_square = jnp.mean(stream * stream, axis=-1, keepdims=True)
        normed_own = (stream * lax.rsqrt(mean_square + 1e-05) * norm_gain).astype(jnp.bfloat16)
        normed_own, weights_peer = lax.optimization_barrier((normed_own, weights_peer))
        normed = lax.all_gather(
            normed_own, "exp", axis=0, tiled=True, axis_index_groups=columns
        )
        cores = [[CORES * i + c for c in range(CORES)] for i in range(chips)]
        normed = lax.all_gather(normed, "exp", axis=0, tiled=True, axis_index_groups=cores)

    with jax.named_scope("dispatch"):
        outgoing = run_select(selector, normed).reshape(seq_devices, chunks * share, CHUNK)
        arrived = lax.all_to_all(outgoing, "seq", split_axis=0, concat_axis=0, tiled=True)

    with jax.named_scope("experts"):
        chunk_rows = arrived.reshape(seq_devices * chunks * share, CHUNK)
        start = run_peer(chunk_rows, weights_peer)
        done = run_expert(chunk_rows, start, weights)

    with jax.named_scope("combine"):
        returned = lax.all_to_all(
            done.reshape(seq_devices, chunks * share, CHUNK),
            "seq",
            split_axis=0,
            concat_axis=0,
            tiled=True,
        )
        term = run_combine(
            combiner, returned.reshape(seq_devices * chunks * share, CHUNK), width
        )
        terms = lax.all_to_all(
            term.reshape(exp_devices, own_rows, width),
            "exp",
            split_axis=0,
            concat_axis=0,
            tiled=True,
        )
        expert_sum = jnp.sum(terms.astype(jnp.float32), axis=0)
        layer_out = (residual.astype(jnp.float32) + expert_sum).astype(jnp.bfloat16)
    return layer_out[None]


def solution(mesh):
    placed = (
        P("batch", "seq", "exp"),
        P("batch", "seq", "exp"),
        P("exp"),
        P("exp", None),
        P("batch", ("seq", "exp"), None),
        P(),
        P("batch", "seq", None),
        P("batch", "seq", None),
        P("seq", None, "exp"),
        P("seq", None, "exp"),
        P("seq", "exp", None),
    )
    return jax.shard_map(
        on_device,
        mesh=mesh,
        in_specs=placed,
        out_specs=P("batch", ("seq", "exp"), None),
        check_vma=False,
    )
```

```python
import jax
import jax.numpy as jnp
from jax import lax
from jax.experimental import pallas as pl
from jax.experimental.pallas import tpu as pltpu
from jax.sharding import PartitionSpec as P

HEAD = 64
TILE = 16
LANES = 128
CHUNK = 384
CAP = 24
GROUP = 24
CORES = 2
RUN = 16


def pack_kernel(
    gate_ref, up_ref, down_ref, out_ref, gate_vmem, up_vmem, down_vmem, packed_ref, sems, out_sems
):
    width = gate_ref.shape[1]
    half = up_ref.shape[0] // 2
    low = width // LANES * LANES
    pairs = ((gate_ref, gate_vmem), (up_ref, up_vmem), (down_ref, down_vmem))
    loads = [pltpu.make_async_copy(s, d, sems.at[i]) for i, (s, d) in enumerate(pairs)]
    spans = (slice(0, low), slice(low, 2 * width))
    stores = [
        pltpu.make_async_copy(packed_ref.at[:, span], out_ref.at[:, span], out_sems.at[i])
        for i, span in enumerate(spans)
    ]
    for load in loads:
        load.start()
    loads[0].wait()
    loads[1].wait()
    up = up_vmem[...]
    left = jnp.concatenate([gate_vmem[...], up[:half]], axis=0)
    packed_ref[:, :low] = left[:, :low]
    stores[0].start()
    loads[2].wait()
    right = jnp.concatenate([up[half:], down_vmem[...]], axis=0)
    packed_ref[:, low:] = jnp.concatenate([left[:, low:], right], axis=1)
    stores[1].start()
    for store in stores:
        store.wait()


def pack_weights(gate_across, up_across, down):
    units, width = down.shape
    packed = (3 * units // 2, 2 * width)
    return pl.pallas_call(
        pack_kernel,
        in_specs=[pl.BlockSpec(memory_space=pl.ANY)] * 3,
        out_specs=pl.BlockSpec(memory_space=pl.ANY),
        out_shape=jax.ShapeDtypeStruct(packed, down.dtype),
        scratch_shapes=[pltpu.VMEM(down.shape, down.dtype)] * 3
        + [
            pltpu.VMEM(packed, down.dtype),
            pltpu.SemaphoreType.DMA((3,)),
            pltpu.SemaphoreType.DMA((2,)),
        ],
        compiler_params=pltpu.CompilerParams(vmem_limit_bytes=56 * 1024 * 1024),
        cost_estimate=pl.CostEstimate(
            flops=0, bytes_accessed=12 * units * width, transcendentals=0
        ),
    )(gate_across, up_across, down)


def chunk_turn(chunks, back):
    side = GROUP * chunks
    share = CAP // chunks
    row = lax.broadcasted_iota(jnp.int32, (side, side), 1 if back else 0)
    col = lax.broadcasted_iota(jnp.int32, (side, side), 0 if back else 1)
    block, rest = row // (chunks * share), row % (chunks * share)
    source = (rest // share) * GROUP + block * share + rest % share
    return (source == col).astype(jnp.bfloat16)


def store_chunks(rows_ref, out_ref):
    count, width = rows_ref.shape
    chunks = out_ref.shape[0] // count
    turn = chunk_turn(chunks, False)
    for first in range(0, count, GROUP):
        pieces = []
        for chunk in range(chunks):
            low, high = chunk * CHUNK, min((chunk + 1) * CHUNK, width)
            piece = rows_ref[first : first + GROUP, low:high]
            if high - low < CHUNK:
                fill = jnp.zeros((GROUP, CHUNK - (high - low)), piece.dtype)
                piece = jnp.concatenate([piece, fill], axis=1)
            pieces.append(piece)
        stacked = jnp.concatenate(pieces, axis=0).astype(jnp.bfloat16)
        out_ref[first * chunks : (first + GROUP) * chunks, :] = jnp.dot(
            turn, stacked, preferred_element_type=jnp.float32
        ).astype(out_ref.dtype)


def load_chunks(chunks_ref, count):
    chunks = chunks_ref.shape[0] // count
    turn = chunk_turn(chunks, True)
    rows = []
    for first in range(0, count, GROUP):
        stacked = jnp.dot(
            turn,
            chunks_ref[first * chunks : (first + GROUP) * chunks, :],
            preferred_element_type=jnp.float32,
        )
        rows.append(
            jnp.concatenate([stacked[i * GROUP : (i + 1) * GROUP] for i in range(chunks)], axis=1)
        )
    return jnp.concatenate(rows, axis=0)


def combine_kernel(combiner_ref, chunks_ref, out_ref):
    width = out_ref.shape[1]
    rows = load_chunks(chunks_ref, combiner_ref.shape[1])[:, :width].astype(jnp.bfloat16)
    out_ref[...] = jnp.dot(
        combiner_ref[...], rows, preferred_element_type=jnp.float32
    ).astype(out_ref.dtype)


def run_combine(combiner, chunk_rows, width):
    tokens, count = combiner.shape
    return pl.pallas_call(
        combine_kernel,
        out_shape=jax.ShapeDtypeStruct((tokens, width), jnp.bfloat16),
        compiler_params=pltpu.CompilerParams(vmem_limit_bytes=24 * 1024 * 1024),
        cost_estimate=pl.CostEstimate(
            flops=2 * tokens * count * width, bytes_accessed=4 * tokens * width, transcendentals=0
        ),
    )(combiner, chunk_rows)


def select_kernel(selector_ref, normed_ref, out_ref, rows_ref):
    rows_ref[...] = jnp.dot(
        selector_ref[...], normed_ref[...], preferred_element_type=jnp.float32
    )
    store_chunks(rows_ref, out_ref)


def run_select(selector, normed):
    count, depth = selector.shape
    width = normed.shape[1]
    chunks = -(-width // CHUNK)
    return pl.pallas_call(
        select_kernel,
        out_shape=jax.ShapeDtypeStruct((count * chunks, CHUNK), jnp.bfloat16),
        scratch_shapes=[pltpu.VMEM((count, width), jnp.float32)],
        compiler_params=pltpu.CompilerParams(vmem_limit_bytes=24 * 1024 * 1024),
        cost_estimate=pl.CostEstimate(
            flops=4 * count * depth * width, bytes_accessed=4 * count * width, transcendentals=0
        ),
    )(selector, normed)


def pad_across(rows_across):
    width, count = rows_across.shape
    spare = jnp.zeros((-width % LANES, count), rows_across.dtype)
    return (
        jnp.concatenate([rows_across, spare], axis=0),
        jnp.concatenate([spare, rows_across], axis=0),
    )


def group_term(weight_ref, across):
    span, count = across[0].shape
    units = weight_ref.shape[0] * 2 // 3
    half = units // 2
    low = weight_ref.shape[1] - span
    up_rows = -(-half // TILE) * TILE
    down_from = half // TILE * TILE
    cut = units // TILE * TILE
    left = jnp.concatenate(
        [
            jnp.dot(weight_ref[:cut, :span], across[0], preferred_element_type=jnp.float32),
            jnp.dot(weight_ref[cut:, :span], across[0], preferred_element_type=jnp.float32),
        ],
        axis=0,
    )
    right = jnp.dot(weight_ref[:up_rows, low:], across[1], preferred_element_type=jnp.float32)
    gate = left[:units]
    lifted = jnp.concatenate([left[units:], right[:half]], axis=0)
    hidden = gate * jax.nn.sigmoid(1.702 * gate) * (lifted + 1.0)
    lead = jnp.zeros((half - down_from, count), jnp.float32)
    return jnp.dot(
        jnp.concatenate([lead, hidden], axis=0).T.astype(jnp.bfloat16),
        weight_ref[down_from:, low:],
        preferred_element_type=jnp.float32,
    )


def peer_kernel(chunks_ref, peer_ref, total_ref, held_ref, sem):
    count, width = total_ref.shape
    copy = pltpu.make_async_copy(peer_ref, held_ref, sem)
    copy.start()
    rows_across = load_chunks(chunks_ref, count).T[:width].astype(jnp.bfloat16)
    across = pad_across(rows_across)
    copy.wait()
    term = group_term(held_ref, across)
    total_ref[...] = term[:, term.shape[1] - width :]


def run_peer(chunk_rows, peer):
    depth, width = peer.shape[0] * 2, peer.shape[1] // 2
    count = chunk_rows.shape[0] // -(-width // CHUNK)
    return pl.pallas_call(
        peer_kernel,
        in_specs=[
            pl.BlockSpec(memory_space=pltpu.VMEM),
            pl.BlockSpec(memory_space=pl.ANY),
        ],
        out_specs=pl.BlockSpec(memory_space=pltpu.VMEM),
        out_shape=jax.ShapeDtypeStruct((count, width), jnp.float32),
        scratch_shapes=[
            pltpu.VMEM(peer.shape, jnp.bfloat16),
            pltpu.SemaphoreType.DMA,
        ],
        compiler_params=pltpu.CompilerParams(vmem_limit_bytes=24 * 1024 * 1024),
        cost_estimate=pl.CostEstimate(
            flops=2 * count * width * depth,
            bytes_accessed=2 * depth * width,
            transcendentals=count * depth // 3,
        ),
    )(chunk_rows, peer)


def expert_kernel(
    chunks_ref, start_ref, weight_ref, out_ref, held_ref, total_ref, wide_ref, sems
):
    groups = weight_ref.shape[0]
    others = held_ref.shape[0]
    count, width = total_ref.shape
    rank = lax.axis_index("exp")
    first = rank // CORES * CORES + CORES

    def fetch(i):
        group = lax.rem(first + i, groups) if i < groups - CORES else rank
        return pltpu.make_async_copy(weight_ref.at[group], held_ref.at[i], sems.at[i])

    for i in range(others):
        fetch(i).start()
    rows_across = load_chunks(chunks_ref, count).T[:width].astype(jnp.bfloat16)
    across = pad_across(rows_across)
    for i in range(others):
        fetch(i).wait()
        term = group_term(held_ref.at[i], across)
        if i == 0:
            wide_ref[...] = term
        else:
            wide_ref[...] += term
    total_ref[...] = start_ref[...] + wide_ref[:, wide_ref.shape[1] - width :]
    store_chunks(total_ref, out_ref)


def run_expert(chunk_rows, start, weights):
    groups, depth, _ = weights.shape
    count, width = start.shape
    others = groups - 1
    span = -(-width // LANES) * LANES
    return pl.pallas_call(
        expert_kernel,
        in_specs=[
            pl.BlockSpec(memory_space=pltpu.VMEM),
            pl.BlockSpec(memory_space=pltpu.VMEM),
            pl.BlockSpec(memory_space=pl.ANY),
        ],
        out_specs=pl.BlockSpec(memory_space=pltpu.VMEM),
        out_shape=jax.ShapeDtypeStruct(chunk_rows.shape, jnp.bfloat16),
        scratch_shapes=[
            pltpu.VMEM((others,) + weights.shape[1:], jnp.bfloat16),
            pltpu.VMEM((count, width), jnp.float32),
            pltpu.VMEM((count, span), jnp.float32),
            pltpu.SemaphoreType.DMA((others,)),
        ],
        compiler_params=pltpu.CompilerParams(vmem_limit_bytes=44 * 1024 * 1024),
        cost_estimate=pl.CostEstimate(
            flops=4 * count * width * depth * others,
            bytes_accessed=others * depth * width * 4,
            transcendentals=count * depth * others // 2,
        ),
    )(chunk_rows, start, weights)


def on_device(
    queries,
    keys_values,
    sinks,
    out_weight,
    hidden_in,
    norm_gain,
    expert_ids,
    expert_gates,
    gate_weight,
    up_weight,
    down_weight,
):
    seq_devices = lax.axis_size("seq")
    exp_devices = lax.axis_size("exp")
    block_rows = queries.shape[1]
    heads = sinks.shape[0]
    width = out_weight.shape[1]
    own_rows = hidden_in.shape[1]
    units = gate_weight.shape[2]
    seq_rank = lax.axis_index("seq")
    exp_rank = lax.axis_index("exp")
    run_rows = RUN * block_rows
    runs = seq_devices // RUN

    with jax.named_scope("gather_weights"):
        weights_own = pack_weights(gate_weight[0].T, up_weight[0].T, down_weight[0])
        weights = lax.all_gather(weights_own, "exp", axis=0, tiled=False)
        swap = [(i, i ^ 1) for i in range(exp_devices)]
        weights_peer = lax.ppermute(weights_own, "exp", swap)

    with jax.named_scope("gather_keys"):
        run_groups = [[r * RUN + i for i in range(RUN)] for r in range(runs)]
        copies = jnp.broadcast_to(keys_values, (RUN,) + keys_values.shape[1:])
        near = lax.all_to_all(
            copies, "seq", split_axis=0, concat_axis=0, tiled=True, axis_index_groups=run_groups
        )
        near = near.reshape(run_rows, 2 * HEAD)
        to_far = [(i, i + RUN) for i in range(seq_devices - RUN)]
        to_near = [(i + RUN, i) for i in range(seq_devices - RUN)]
        guests = lax.ppermute(queries[0], "seq", to_near)

    with jax.named_scope("route"):
        chips = exp_devices // CORES
        core = exp_rank % CORES
        chosen = expert_ids[0]
        share = CAP // exp_devices
        hits = (chosen[:, :, None] == jnp.arange(seq_devices, dtype=jnp.int32)).astype(jnp.float32)
        token_hits = jnp.sum(hits, axis=1)
        earlier = (
            jnp.arange(block_rows)[:, None] > jnp.arange(block_rows)[None, :]
        ).astype(jnp.float32)
        slots = jnp.dot(earlier, token_hits)
        named = token_hits[:, :, None] > 0
        wanted = (exp_rank * share + jnp.arange(share, dtype=jnp.int32)).astype(jnp.float32)
        picks = named & (slots[:, :, None] == wanted)
        selector = picks.astype(jnp.bfloat16).reshape(
            chips, CORES, own_rows, seq_devices * share
        )
        selector = selector.transpose(3, 1, 0, 2).reshape(seq_devices * share, block_rows)
        factor = jnp.einsum("tke,tk->te", hits, expert_gates[0].astype(jnp.float32))
        combiner = jnp.where(picks, factor[:, :, None], 0.0).astype(jnp.bfloat16)
        chunks = -(-width // CHUNK)
        combiner = combiner.reshape(block_rows, seq_devices * share)
        selector, combiner, near = lax.optimization_barrier((selector, combiner, near))

    with jax.named_scope("attend"):
        own_pos = (seq_rank % RUN) * block_rows + jnp.arange(block_rows, dtype=jnp.int32)
        key_pos = jnp.arange(run_rows, dtype=jnp.int32)

        def attend(rows, allowed):
            scores = (
                jnp.einsum(
                    "igd,jd->gij",
                    rows.reshape(block_rows, heads, HEAD),
                    near[:, :HEAD],
                    preferred_element_type=jnp.float32,
                )
                * 0.125
            )
            if allowed is not None:
                scores = jnp.where(allowed, scores, -1e30)
            top = jnp.max(scores, axis=-1)
            numerators = jnp.exp(scores - top[..., None])
            mix = jnp.einsum(
                "gij,jd->gid",
                numerators.astype(jnp.bfloat16),
                near[:, HEAD:],
                preferred_element_type=jnp.float32,
            )
            return top, jnp.sum(numerators, axis=-1), mix

        guest_top, guest_sum, guest_mix = attend(guests, None)
        far_mix = lax.ppermute(guest_mix.astype(jnp.bfloat16), "seq", to_far)
        far_stats = lax.ppermute(jnp.stack([guest_top, guest_sum]), "seq", to_far)
        top, sums, weighted = attend(queries[0], key_pos[None, :] <= own_pos[:, None])
        far_top = jnp.where(seq_rank >= RUN, far_stats[0], -1e30)
        largest = jnp.maximum(jnp.maximum(top, far_top), sinks[:, None])
        near_scale = jnp.exp(top - largest)
        far_scale = jnp.exp(far_top - largest)
        totals = (
            sums * near_scale + far_stats[1] * far_scale + jnp.exp(sinks[:, None] - largest)
        )
        weighted = (
            weighted * near_scale[..., None]
            + far_mix.astype(jnp.float32) * far_scale[..., None]
        )
        mixed = (weighted / totals[..., None]).astype(jnp.bfloat16)
        heads_out = mixed.transpose(1, 0, 2).reshape(block_rows, heads * HEAD)

    with jax.named_scope("project"):
        head_term = jnp.dot(heads_out, out_weight, preferred_element_type=jnp.float32)
        head_parts = head_term.reshape(chips, CORES, own_rows, width)
        given = lax.dynamic_index_in_dim(head_parts, 1 - core, 1, keepdims=False)
        kept = lax.dynamic_index_in_dim(head_parts, core, 1, keepdims=False)
        taken = lax.ppermute(given.astype(jnp.bfloat16), "exp", swap)
        pair = (kept + taken.astype(jnp.float32)).astype(jnp.bfloat16)
        columns = [[CORES * i + c for i in range(chips)] for c in range(CORES)]
        own_parts = lax.all_to_all(
            pair, "exp", split_axis=0, concat_axis=0, tiled=True, axis_index_groups=columns
        )
        attention = jnp.sum(own_parts.astype(jnp.float32), axis=0)
        residual = (hidden_in[0].astype(jnp.float32) + attention).astype(jnp.bfloat16)

    with jax.named_scope("norm"):
        stream = residual.astype(jnp.float32)
        mean_square = jnp.mean(stream * stream, axis=-1, keepdims=True)
        normed_own = (stream * lax.rsqrt(mean_square + 1e-05) * norm_gain).astype(jnp.bfloat16)
        normed_own, weights_peer = lax.optimization_barrier((normed_own, weights_peer))
        normed = lax.all_gather(
            normed_own, "exp", axis=0, tiled=True, axis_index_groups=columns
        )
        cores = [[CORES * i + c for c in range(CORES)] for i in range(chips)]
        normed = lax.all_gather(normed, "exp", axis=0, tiled=True, axis_index_groups=cores)

    with jax.named_scope("dispatch"):
        outgoing = run_select(selector, normed).reshape(seq_devices, chunks * share, CHUNK)
        arrived = lax.all_to_all(outgoing, "seq", split_axis=0, concat_axis=0, tiled=True)

    with jax.named_scope("experts"):
        chunk_rows = arrived.reshape(seq_devices * chunks * share, CHUNK)
        start = run_peer(chunk_rows, weights_peer)
        done = run_expert(chunk_rows, start, weights)

    with jax.named_scope("combine"):
        returned = lax.all_to_all(
            done.reshape(seq_devices, chunks * share, CHUNK),
            "seq",
            split_axis=0,
            concat_axis=0,
            tiled=True,
        )
        term = run_combine(
            combiner, returned.reshape(seq_devices * chunks * share, CHUNK), width
        )
        terms = lax.all_to_all(
            term.reshape(exp_devices, own_rows, width),
            "exp",
            split_axis=0,
            concat_axis=0,
            tiled=True,
        )
        expert_sum = jnp.sum(terms.astype(jnp.float32), axis=0)
        layer_out = (residual.astype(jnp.float32) + expert_sum).astype(jnp.bfloat16)
    return layer_out[None]


def solution(mesh):
    placed = (
        P("batch", "seq", "exp"),
        P("batch", "seq", "exp"),
        P("exp"),
        P("exp", None),
        P("batch", ("seq", "exp"), None),
        P(),
        P("batch", "seq", None),
        P("batch", "seq", None),
        P("seq", None, "exp"),
        P("seq", None, "exp"),
        P("seq", "exp", None),
    )
    return jax.shard_map(
        on_device,
        mesh=mesh,
        in_specs=placed,
        out_specs=P("batch", ("seq", "exp"), None),
        check_vma=False,
    )
```
